128 devices in a mesh: seq: 32 (over z, x_lo, y), head: 4 (over x_hi, core).
Axes of the slice: x: 4 (x_hi: 2, x_lo: 2; x = x_hi * 2 + x_lo), y: 4, z: 4, core: 2. Of those that a mesh axis runs over, the one named last changes fastest.
Arguments:
- queries: bfloat16 [2, 4096, 3584], P(None, 'seq', 'head')
- fine_keys: bfloat16 [2, 4096, 3584], P(None, 'seq', 'head')
- fine_values: bfloat16 [2, 4096, 3584], P(None, 'seq', 'head'), may hold values from -48 to 48
- cache_keys: bfloat16 [2, 1024, 3584], P(None, ('seq', 'head')), may hold values from -6 to 6
- cache_values: bfloat16 [2, 1024, 3584], P(None, ('seq', 'head')), may hold values from -48 to 48
- prefix_len: int32 [2], replicated, may hold values from 512 to 1024, as said below
- out_weight: bfloat16 [3584, 3584], P('head'), may hold values from -0.375 to 0.375
Outputs:
- projected: bfloat16 [2, 4096, 3584], P(None, 'seq', 'head')
The draws below stay inside these ranges and needn't reach their ends.
Inputs may be any that keep to these rules, and one draw needn't show every extreme that they name: `prefix_len`: the first request sees all 1024 cached tokens.
All inputs are finite; a program needn't handle non-finite values.
Results may differ from the reference program's by a relative error of at most 0.015.
Values may be sent and summed in bfloat16 or wider, within the bound.
A program may use at most 192 MiB of HBM per device.

```python
import jax
import jax.numpy as jnp
from jax import lax

H = 28
HD = 128
D = 3584
REQS = 2
FINE = 4096
COARSE = 1024


def draw_queries(key, part):
    key = jax.random.fold_in(key, 11)
    result = jax.random.normal(key, (REQS, FINE, D), jnp.float32)
    return result.astype(jnp.bfloat16)


def draw_fine_keys(key, part):
    key = jax.random.fold_in(key, 12)
    result = jax.random.normal(key, (REQS, FINE, D), jnp.float32)
    return result.astype(jnp.bfloat16)


def draw_prefix_len(key, part):
    key = jax.random.fold_in(key, 13)
    lengths = jax.random.randint(key, (REQS,), COARSE // 2, COARSE + 1, dtype=jnp.int32)
    return lengths.at[0].set(COARSE)


def levels(rng, extent, pieces, least, high):
    level = 1.0
    for axis_at, blocks in pieces:
        draws = jax.random.uniform(jax.random.fold_in(jax.random.fold_in(rng, 6), axis_at), (blocks,), jnp.float32, least / len(pieces), high / len(pieces))
        level = level * jnp.repeat(jnp.exp(draws), extent[axis_at] // blocks).reshape((-1,) + (1,) * (len(extent) - 1 - axis_at))
    return level


def bell_draw(own_key, shape, width, limit, cuts=(), kind=jnp.bfloat16):
    entries = jax.random.normal(own_key, shape, jnp.float32) * width
    if len(cuts) > 0:
        entries = levels(own_key, shape, cuts, -0.22, 0.18) * entries
    return jnp.clip(entries, min=-limit, max=limit).astype(kind)


def setup_inputs(seed: int = 0) -> dict:
    keys = jax.random.split(jax.random.key(seed), 8)
    return {
        "queries": draw_queries(jax.random.fold_in(keys[7], 71), 0),
        "fine_keys": draw_fine_keys(jax.random.fold_in(keys[7], 71), 0),
        "fine_values": bell_draw(keys[2], (REQS, FINE, D), 8.0, 48.0, ((1, 32), (2, 4))),
        "cache_keys": bell_draw(keys[3], (REQS, COARSE, D), 1.0, 6.0, ((1, 128),)),
        "cache_values": bell_draw(keys[4], (REQS, COARSE, D), 8.0, 48.0, ((1, 128),)),
        "prefix_len": draw_prefix_len(jax.random.fold_in(keys[7], 71), 0),
        "out_weight": bell_draw(keys[6], (D, D), (D // 16) ** -0.5, 0.375, ((0, 4),)),
    }


def attend_head(query_head, key_head, value_head, visible):
    scores = jnp.dot(query_head, key_head.T, preferred_element_type=jnp.float32) * (HD ** -0.5)
    scores = jnp.where(visible[None, :], scores, jnp.float32(-1e30))
    row_max = jnp.max(scores, axis=1, keepdims=True)
    weights = jnp.where(visible[None, :], jnp.exp(scores - row_max), jnp.float32(0.0))
    total = jnp.sum(weights, axis=1, keepdims=True)
    summed = jnp.dot(weights.astype(jnp.bfloat16), value_head, preferred_element_type=jnp.float32)
    return (summed / total).astype(jnp.bfloat16)


def reference(queries, fine_keys, fine_values, cache_keys, cache_values, prefix_len, out_weight):
    positions = jnp.arange(COARSE + FINE, dtype=jnp.int32)
    attended_all = []
    for request in range(REQS):
        visible = (positions >= COARSE) | (positions < prefix_len[request])
        key_all = jnp.concatenate([cache_keys[request], fine_keys[request]], axis=0)
        value_all = jnp.concatenate([cache_values[request], fine_values[request]], axis=0)
        query_heads = queries[request].reshape(FINE, H, HD).transpose(1, 0, 2)
        key_heads = key_all.reshape(COARSE + FINE, H, HD).transpose(1, 0, 2)
        value_heads = value_all.reshape(COARSE + FINE, H, HD).transpose(1, 0, 2)
        outputs = lax.map(lambda trio: attend_head(trio[0], trio[1], trio[2], visible), (query_heads, key_heads, value_heads))
        attended_all.append(outputs.transpose(1, 0, 2).reshape(FINE, D))
    attended = jnp.stack(attended_all, axis=0).reshape(REQS * FINE, D)
    projected = jnp.dot(attended, out_weight, preferred_element_type=jnp.float32)
    return projected.astype(jnp.bfloat16).reshape(REQS, FINE, D)
```

```python
import functools

import jax
import jax.numpy as jnp
from jax import lax
from jax.experimental import pallas as pl
from jax.experimental.pallas import tpu as pltpu
from jax.sharding import PartitionSpec as P

MESH = pl.DeviceIdType.MESH
F32, BF = jnp.float32, jnp.bfloat16
HD = 128
HEADS = 7
GW = HEADS * HD
TOK = 128
COARSE = 1024
KEYS = 5120
TQ = 256
CK = 1024
SLOTS = 16
QUART = TOK // 4
PHASES = ((0, 64), (64, 32), (96, 32))
LOG2 = float(HD ** -0.5 * 1.4426950408889634)


def rcopy(src, dst, ssem, rsem, s, g):
    return pltpu.make_async_remote_copy(
        src_ref=src, dst_ref=dst, send_sem=ssem, recv_sem=rsem,
        device_id=(s, g), device_id_type=MESH)


def kernel(q_ref, fk_ref, fv_ref, ck_ref, cv_ref, plen_ref, w_ref, out_ref,
           st1k, st1v, st2k, st2v, kall, vx, kt, qland, sc0, sc1, qx, mx, acc, obuf, att, wv,
           psend, precv, csend,
           st1_ss, st1_rs, k_ss, k_rs, v_ss, v_rs, q_ss, q_rs, fk_ss, fk_rs, fv_ss, fv_rs,
           ck_ss, ck_rs, cv_ss, cv_rs, cf_ss, cf_rs, o_ss, o_rs, p_ss, p_rs, c_ss, c_rs, w_sem):
    s = lax.axis_index("seq")
    g = lax.axis_index("head")
    z, xl, y = s >> 3, (s >> 2) & 1, s & 3
    xh, c = g >> 1, g & 1
    zk = z >> 1
    sib = xh * 2 + 1 - c
    flip = z * 8 + (1 - xl) * 4 + y

    def place(zd, pos):
        return (pos + 8 - 2 * zd) & 7

    def dest(j):
        zb, xb, yb = j >> 3, (j >> 2) & 1, j & 3
        r = (z + zb) & 1
        zd = 2 * c + r
        pos = ((xl + xb) & 1) * 4 + ((y + yb) & 3)
        h = place(zd, pos)
        sd = zd * 8 + pos
        mine = jnp.logical_and(sd == s, zk == c)
        return r, h, sd, mine

    my_r = z & 1
    my_h = place(z, xl * 4 + y)
    active = my_h < HEADS

    def source(j):
        zb, xb, yb = j >> 3, (j >> 2) & 1, j & 3
        zs = 2 * c + ((my_r + zb) & 1)
        return zs, (xl + xb) & 1, (y + 4 - yb) & 3

    barrier = pltpu.get_barrier_semaphore()
    gd = xh * 2 + zk

    def greet(j, carry):
        _, _, sd, mine = dest(j)

        @pl.when(jnp.logical_not(mine))
        def _():
            pl.semaphore_signal(barrier, inc=1, device_id=(sd, gd), device_id_type=MESH)
        return carry
    lax.fori_loop(0, 16, greet, 0)
    for i in range(1, 4):
        pl.semaphore_signal(barrier, inc=1, device_id=(s, (g + i) & 3), device_id_type=MESH)
    for i in range(2):
        pl.semaphore_signal(barrier, inc=1, device_id=(flip, i * 2 + c), device_id_type=MESH)
    wcopy = pltpu.make_async_copy(w_ref, wv, w_sem)
    wcopy.start()
    vx[:, HD:] = jnp.ones((KEYS, HD), BF)
    pl.semaphore_wait(barrier, 21 - jnp.where(zk == c, 1, 0))


    def st1(i, src, dst, n):
        gp = (g + i) & 3
        cols = pl.ds(pl.multiple_of(gp * GW, HD), GW)
        if i == 0:
            return pltpu.make_async_copy(src.at[:, cols], dst.at[g], st1_rs.at[n, 0])
        return rcopy(src.at[:, cols], dst.at[g], st1_ss.at[n, i], st1_rs.at[n, i], s, gp)
    first = [st1(i, src, dst, n) for i in range(4)
             for n, (src, dst) in enumerate(((ck_ref, st1k), (cv_ref, st1v)))]
    for f in first:
        f.start()

    def move(src, dst, ss, rs, sd, mine):
        @pl.when(mine)
        def _():
            pltpu.make_async_copy(src, dst, rs).start()

        @pl.when(jnp.logical_not(mine))
        def _():
            rcopy(src, dst, ss, rs, sd, gd).start()

    has_mine = jnp.logical_and(zk == c, active)

    def sent(piece, n, sem):
        @pl.when(has_mine)
        def _():
            rcopy(piece(n - 1), piece(n - 1), sem, sem, s, sib).wait_send()

        @pl.when(jnp.logical_not(has_mine))
        def _():
            rcopy(piece(n), piece(n), sem, sem, s, sib).wait_send()

    def came(piece, sem):
        rcopy(piece, piece, sem, sem, s, sib).wait_recv()

    def hcols(h):
        return pl.ds(pl.multiple_of(h * HD, HD), HD)

    def krows(slot, n=1):
        return pl.ds(pl.multiple_of(COARSE + slot * TOK, TOK), n * TOK)

    def kv_args(j):
        r, h, sd, mine = dest(j)
        rows = krows(zk * 16 + j)
        return (h, (fk_ref.at[r, :, hcols(h)], kall.at[rows, :], k_ss, k_rs.at[j >> 2], sd, mine),
                (fv_ref.at[r, :, hcols(h)], vx.at[rows, 0:HD], v_ss, v_rs.at[j >> 2], sd, mine))

    def q_args(part):
        rows = pl.ds(0, QUART) if part == 0 else pl.ds(QUART, TOK - QUART)

        def args(j):
            r, h, sd, mine = dest(j)
            return h, (q_ref.at[r, rows, hcols(h)], qland.at[j, rows, :],
                       q_ss.at[part], q_rs.at[part, j >> 3], sd, mine)
        return args

    def c_args(j):
        r, h, sd, mine = dest(j)
        rows = pl.ds(pl.multiple_of(s * 32, 32), 32)
        return (h, (st2k.at[r, :, hcols(h)], kall.at[rows, :], ck_ss, ck_rs, sd, mine),
                (st2v.at[r, :, hcols(h)], vx.at[rows, 0:HD], cv_ss, cv_rs, sd, mine))

    def each(args, what):
        def step(j, carry):
            h, *copies = args(j)

            @pl.when(h < HEADS)
            def _():
                for a in copies:
                    what(*a)
            return carry
        lax.fori_loop(0, 16, step, 0)

    each(kv_args, move)

    for i in range(4):
        for n, (src, dst) in enumerate(((ck_ref, st1k), (cv_ref, st1v))):
            if i == 0:
                st1(0, src, dst, n).wait()
            else:
                st1(i, src, dst, n).wait_recv()
    for r in range(2):
        for a in range(2):
            for src, dst in ((st1k, st2k), (st1v, st2v)):
                lo = src[2 * a].astype(F32)[r * 8:r * 8 + 8]
                hi = src[2 * a + 1].astype(F32)[r * 8:r * 8 + 8]
                dst[r, a * 16:a * 16 + 16, :] = jnp.concatenate([lo, hi], axis=0).astype(BF)
    each(c_args, move)
    each(q_args(0), move)

    ohead = pl.multiple_of(my_h * HD, HD)
    go = xh * 2 + zk

    def o_args(ph, j):
        zs, xs, ys = source(j)
        so = zs * 8 + (1 - xs) * 4 + ys
        rows = pl.ds(*PHASES[ph])
        mine = jnp.logical_and(so == s, zk == c)
        return (obuf.at[j, rows, :], att.at[my_r, rows, pl.ds(ohead, HD)], o_ss.at[ph],
                o_rs.at[ph], so, mine)

    def give_back(ph, first, count):
        def step(j, carry):
            move(*o_args(ph, j))
            return carry
        lax.fori_loop(first, first + count, step, 0)

    def fwd(ref_k, ss, rs, i, owner, is_v):
        rows = krows(owner * 16 + i * 4, 4)
        piece = ref_k.at[rows, 0:HD] if is_v else ref_k.at[rows, :]
        return rcopy(piece, piece, ss.at[i], rs.at[i], s, sib)

    def cfwd(ref_k, n, owner, is_v):
        rows = pl.ds(pl.multiple_of(owner * 512, 512), 512)
        piece = ref_k.at[rows, 0:HD] if is_v else ref_k.at[rows, :]
        return rcopy(piece, piece, cf_ss.at[n], cf_rs.at[n], s, sib)

    def transpose(row):
        for b in range(2):
            rows = pl.ds(pl.multiple_of(row + b * 256, 256), 256)
            kk = kall[rows, :].T
            kt[0:HD, rows] = kk
            kt[HD:, rows] = kk

    @pl.when(active)
    def _():
        def landed(i, carry):
            rows = krows(c * 16 + i * 4, 4)
            came(kall.at[rows, :], k_rs.at[i])
            fwd(kall, fk_ss, fk_rs, i, c, False).start()
            came(vx.at[rows, 0:HD], v_rs.at[i])
            fwd(vx, fv_ss, fv_rs, i, c, True).start()
            return carry
        lax.fori_loop(0, 4, landed, 0)
        rows = pl.ds(pl.multiple_of(c * 512, 512), 512)
        came(kall.at[rows, :], ck_rs)
        cfwd(kall, 0, c, False).start()
        came(vx.at[rows, 0:HD], cv_rs)
        cfwd(vx, 1, c, True).start()

    sent(lambda n: kall.at[0:n * TOK, :], 14, k_ss)
    sent(lambda n: kall.at[0:n * TOK, :], 14, v_ss)
    each(q_args(1), move)

    @pl.when(active)
    def _():
        def mine_t(i, carry):
            transpose(COARSE + c * 2048 + i * 512)
            return carry
        lax.fori_loop(0, 4, mine_t, 0)

        def theirs_t(i, carry):
            fwd(kall, fk_ss, fk_rs, i, 1 - c, False).wait_recv()
            transpose(COARSE + (1 - c) * 2048 + i * 512)
            return carry
        lax.fori_loop(0, 4, theirs_t, 0)

        def theirs_v(i, carry):
            fwd(vx, fv_ss, fv_rs, i, 1 - c, True).wait_recv()
            fwd(kall, fk_ss, fk_rs, i, c, False).wait_send()
            fwd(vx, fv_ss, fv_rs, i, c, True).wait_send()
            return carry
        lax.fori_loop(0, 4, theirs_v, 0)
        cfwd(kall, 0, 1 - c, False).wait_recv()
        cfwd(vx, 1, 1 - c, True).wait_recv()
        cfwd(kall, 0, c, False).wait_send()
        cfwd(vx, 1, c, True).wait_send()

        plen = plen_ref[my_r]
        k0 = kall[COARSE:COARSE + 1, :].astype(F32)
        transpose(0)
        for i in range(2, 4):
            rows = slice(i * 256, (i + 1) * 256)
            seen = (lax.broadcasted_iota(jnp.int32, (256, HD), 0) + i * 256) < plen
            kk = jnp.where(seen, kall[rows, :].astype(F32), k0).astype(BF).T
            kt[0:HD, rows] = kk
            kt[HD:, rows] = kk
            vx[rows, 0:HD] = jnp.where(seen, vx[rows, 0:HD].astype(F32), 0.0).astype(BF)
            vx[rows, HD:] = jnp.where(seen, 1.0, 0.0).astype(BF)

    def part(ph, gp):
        r0, n = PHASES[ph]
        rows = jnp.concatenate([att[0, r0:r0 + n, :], att[1, r0:r0 + n, :]], axis=0)
        cols = pl.ds(pl.multiple_of(gp * GW, HD), GW)
        return jnp.dot(rows, wv[:, cols], preferred_element_type=F32)

    def pcopy(ph, i):
        rows = pl.ds(2 * PHASES[ph][0], 2 * PHASES[ph][1])
        return rcopy(psend.at[i, rows, :], precv.at[i, rows, :], p_ss.at[ph, i], p_rs.at[ph, i], s, sib)

    def ccopy(ph, i, half):
        rows = pl.ds(*PHASES[ph])
        return rcopy(csend.at[i, :, rows, :], out_ref.at[half, :, rows, :], c_ss.at[ph, i],
                     c_rs.at[ph, half], flip, i * 2 + c)

    def give(ph):
        r0, n = PHASES[ph]

        came(att.at[:, pl.ds(r0, n), :], o_rs.at[ph])
        if ph == 0:
            wcopy.wait()

        def step(i, carry):
            psend[i, 2 * r0:2 * (r0 + n), :] = part(ph, i * 2 + 1 - c).astype(BF)
            pcopy(ph, i).start()
            return carry
        lax.fori_loop(0, 2, step, 0)

    def take(ph):
        r0, n = PHASES[ph]

        def step(i, carry):
            val = part(ph, i * 2 + c)
            pcopy(ph, i).wait_recv()
            val = (val + precv[i, 2 * r0:2 * (r0 + n), :].astype(F32)).astype(BF)
            for r in range(2):
                csend[i, r, r0:r0 + n, :] = val[r * n:(r + 1) * n]
            ccopy(ph, i, xh).start()
            return carry
        lax.fori_loop(0, 2, step, 0)

    scs = (sc0, sc1)

    def prep(quart, half):
        slots = pl.ds(half * 8, 8)

        @pl.when(quart == 0)
        def _():
            came(qland.at[slots, pl.ds(0, QUART), :], q_rs.at[0, half])

        @pl.when(quart == 1)
        def _():
            came(qland.at[slots, pl.ds(QUART, TOK - QUART), :], q_rs.at[1, half])
        rows = pl.ds(pl.multiple_of(quart * QUART, QUART), QUART)
        x = qland[half * 8:half * 8 + 8, rows, :].reshape(TQ, HD).astype(F32) * LOG2
        hi = x.astype(BF)
        qx[:, :HD] = hi
        qx[:, HD:] = (x - hi.astype(F32)).astype(BF)
        mx[...] = jnp.full((TQ, HD), -jnp.inf, F32)

    def qk(ci, sc):
        cols = slice(ci * CK, (ci + 1) * CK)
        val = jnp.dot(qx[...], kt[:, cols], preferred_element_type=F32)
        sc[:, cols] = val
        m = mx[...]
        for b in range(CK // HD):
            m = jnp.maximum(m, val[:, b * HD:(b + 1) * HD])
        mx[...] = m

    def pv(ci, sc, mrow):
        cols = slice(ci * CK, (ci + 1) * CK)
        p = jnp.exp2(sc[:, cols] - mrow).astype(BF)
        acc[...] += jnp.dot(p, vx[cols, :], preferred_element_type=F32)

    def tile(quart, half, final=False):
        mrow = jnp.max(mx[...], axis=1, keepdims=True)
        acc[...] = jnp.zeros((TQ, 2 * HD), F32)
        if not final:
            prep(quart + half, 1 - half)
        for ci in range(KEYS // CK):
            if not final:
                qk(ci, scs[1 - half])
            pv(ci, scs[half], mrow)
        o = (acc[:, :HD] / acc[:, HD:]).astype(BF)
        rows = pl.ds(pl.multiple_of(quart * QUART, QUART), QUART)
        obuf[half * 8:half * 8 + 8, rows, :] = o.reshape(8, QUART, HD)

    @pl.when(active)
    def _():
        prep(0, 0)
        for ci in range(KEYS // CK):
            qk(ci, sc0)

    def quarter(quart, carry):
        @pl.when(active)
        def _():
            tile(quart, 0)

            @pl.when(quart == 2)
            def _():
                give_back(1, 0, 8)
            tile(quart, 1)

            @pl.when(quart == 1)
            def _():
                give_back(0, 0, 16)

            @pl.when(quart == 2)
            def _():
                give_back(1, 8, 8)
        return carry
    lax.fori_loop(0, 3, quarter, 0)
    give(0)

    @pl.when(active)
    def _():
        tile(3, 0)
        give_back(2, 0, 8)
    take(0)

    @pl.when(active)
    def _():
        tile(3, 1, True)
        give_back(2, 8, 8)
    give(1)
    take(1)
    for i in range(1, 4):
        for n, (src, dst) in enumerate(((ck_ref, st1k), (cv_ref, st1v))):
            st1(i, src, dst, n).wait_send()
    sent(lambda n: kall.at[0:n * 32, :], 14, ck_ss)
    sent(lambda n: kall.at[0:n * 32, :], 14, cv_ss)
    sent(lambda n: qland.at[0:n, pl.ds(0, QUART), :], 14, q_ss.at[0])
    sent(lambda n: qland.at[0:n, pl.ds(QUART, TOK - QUART), :], 14, q_ss.at[1])
    give(2)
    take(2)

    @pl.when(active)
    def _():
        for ph in range(len(PHASES)):
            sent(lambda n: obuf.at[0:n, pl.ds(*PHASES[ph]), :], 16, o_ss.at[ph])
    for ph in range(len(PHASES)):
        for i in range(2):
            pcopy(ph, i).wait_send()
            ccopy(ph, i, xh).wait_send()
    for ph in range(len(PHASES)):
        for i in range(2):
            ccopy(ph, i, i).wait_recv()


def per_device(queries, fine_keys, fine_values, cache_keys, cache_values, prefix_len, out_weight):
    dma = pltpu.SemaphoreType.DMA
    any_spec = pl.BlockSpec(memory_space=pl.ANY)
    halves = pl.pallas_call(
        kernel,
        out_shape=jax.ShapeDtypeStruct((2, 2, TOK, GW), BF),
        in_specs=[any_spec] * 5 + [pl.BlockSpec(memory_space=pltpu.SMEM), any_spec],
        out_specs=any_spec,
        scratch_shapes=[
            pltpu.VMEM((4, 16, GW), BF), pltpu.VMEM((4, 16, GW), BF),
            pltpu.VMEM((2, 32, GW), BF), pltpu.VMEM((2, 32, GW), BF),
            pltpu.VMEM((KEYS, HD), BF), pltpu.VMEM((KEYS, 2 * HD), BF),
            pltpu.VMEM((2 * HD, KEYS), BF), pltpu.VMEM((SLOTS, TOK, HD), BF),
            pltpu.VMEM((TQ, KEYS), F32), pltpu.VMEM((TQ, KEYS), F32),
            pltpu.VMEM((TQ, 2 * HD), BF), pltpu.VMEM((TQ, HD), F32),
            pltpu.VMEM((TQ, 2 * HD), F32), pltpu.VMEM((SLOTS, TOK, HD), BF),
            pltpu.VMEM((2, TOK, GW), BF), pltpu.VMEM((GW, 4 * GW), BF),
            pltpu.VMEM((2, 2 * TOK, GW), BF), pltpu.VMEM((2, 2 * TOK, GW), BF),
            pltpu.VMEM((2, 2, TOK, GW), BF),
            dma((2, 4)), dma((2, 4)), dma, dma((4,)), dma, dma((4,)),
            dma((2,)), dma((2, 2)), dma((4,)), dma((4,)), dma((4,)), dma((4,)),
            dma, dma, dma, dma, dma((2,)), dma((2,)),
            dma((3,)), dma((3,)), dma((3, 2)), dma((3, 2)), dma((3, 2)), dma((3, 2)), dma,
        ],
        compiler_params=pltpu.CompilerParams(
            collective_id=0, has_side_effects=True, vmem_limit_bytes=58 * 2**20),
        cost_estimate=pl.CostEstimate(flops=7_000_000_000, bytes_accessed=12_000_000, transcendentals=10_000_000),
    )(queries, fine_keys, fine_values, cache_keys.reshape(16, 4 * GW),
      cache_values.reshape(16, 4 * GW), prefix_len, out_weight)
    return (halves[0].astype(F32) + halves[1].astype(F32)).astype(BF)


def solution(mesh):
    return jax.shard_map(
        per_device,
        mesh=mesh,
        in_specs=(
            P(None, "seq", "head"),
            P(None, "seq", "head"),
            P(None, "seq", "head"),
            P(None, ("seq", "head"), None),
            P(None, ("seq", "head"), None),
            P(),
            P("head", None),
        ),
        out_specs=P(None, "seq", "head"),
        check_vma=False,
    )
```

```python
import functools

import jax
import jax.numpy as jnp
from jax import lax
from jax.experimental import pallas as pl
from jax.experimental.pallas import tpu as pltpu
from jax.sharding import PartitionSpec as P

MESH = pl.DeviceIdType.MESH
F32, BF = jnp.float32, jnp.bfloat16
HD = 128
HEADS = 7
GW = HEADS * HD
TOK = 128
COARSE = 1024
KEYS = 5120
TQ = 256
CK = 1024
SLOTS = 16
QUART = TOK // 4
PHASES = ((0, 32), (32, 64), (96, 32))
LOG2 = float(HD ** -0.5 * 1.4426950408889634)


def rcopy(src, dst, ssem, rsem, s, g):
    return pltpu.make_async_remote_copy(
        src_ref=src, dst_ref=dst, send_sem=ssem, recv_sem=rsem,
        device_id=(s, g), device_id_type=MESH)


def kernel(q_ref, fk_ref, fv_ref, ck_ref, cv_ref, plen_ref, w_ref, out_ref,
           st1k, st1v, st2k, st2v, kall, vx, kt, qland, sc0, sc1, qx, mx, acc, obuf, att, wv,
           psend, precv, csend,
           st1_ss, st1_rs, k_ss, k_rs, v_ss, v_rs, q_ss, q_rs, fk_ss, fk_rs, fv_ss, fv_rs,
           ck_ss, ck_rs, cv_ss, cv_rs, cf_ss, cf_rs, o_ss, o_rs, p_ss, p_rs, c_ss, c_rs, w_sem):
    s = lax.axis_index("seq")
    g = lax.axis_index("head")
    z, xl, y = s >> 3, (s >> 2) & 1, s & 3
    xh, c = g >> 1, g & 1
    zk = z >> 1
    land = y & 1
    sib = xh * 2 + 1 - c
    flip = z * 8 + (1 - xl) * 4 + y

    def place(zd, pos):
        return (pos + 8 - 2 * zd) & 7

    def dest(j):
        zb, xb, yb = j >> 3, (j >> 2) & 1, j & 3
        r = (z + zb) & 1
        zd = 2 * c + r
        pos = ((xl + xb) & 1) * 4 + ((y + yb) & 3)
        h = place(zd, pos)
        sd = zd * 8 + pos
        mine = jnp.logical_and(sd == s, land == c)
        return r, h, sd, mine

    my_r = z & 1
    my_h = place(z, xl * 4 + y)
    active = my_h < HEADS

    def slot_of(j):
        return (z >> 1) * 8 + (j >> 3) * 4 + ((j >> 2) & 1) * 2 + ((j & 3) >> 1)

    def source(slot):
        zs = (slot >> 3) * 2 + ((my_r + (slot >> 2)) & 1)
        yb = (slot & 1) * 2 + ((y + c) & 1)
        return zs, (xl + (slot >> 1)) & 1, (y + 4 - yb) & 3

    barrier = pltpu.get_barrier_semaphore()
    gd = xh * 2 + land
    go = xh * 2 + zk

    def greet(j, carry):
        _, _, sd, mine = dest(j)
        zs, xs, ys = source(j)
        ss = zs * 8 + xs * 4 + ys

        @pl.when(jnp.logical_not(mine))
        def _():
            pl.semaphore_signal(barrier, inc=1, device_id=(sd, gd), device_id_type=MESH)

        @pl.when(jnp.logical_not(jnp.logical_and(ss == s, zk == c)))
        def _():
            pl.semaphore_signal(barrier, inc=1, device_id=(ss, go), device_id_type=MESH)
        return carry
    lax.fori_loop(0, 16, greet, 0)
    own = jnp.logical_and(zk == c, land == c)
    for i in range(1, 4):
        pl.semaphore_signal(barrier, inc=1, device_id=(s, (g + i) & 3), device_id_type=MESH)
    for i in range(2):
        pl.semaphore_signal(barrier, inc=1, device_id=(flip, i * 2 + c), device_id_type=MESH)
    wcopy = pltpu.make_async_copy(w_ref, wv, w_sem)
    wcopy.start()
    vx[:, HD:] = jnp.ones((KEYS, HD), BF)
    pl.semaphore_wait(barrier, 37 - jnp.where(own, 2, 0))


    def st1(i, src, dst, n):
        gp = (g + i) & 3
        cols = pl.ds(pl.multiple_of(gp * GW, HD), GW)
        if i == 0:
            return pltpu.make_async_copy(src.at[:, cols], dst.at[g], st1_rs.at[n, 0])
        return rcopy(src.at[:, cols], dst.at[g], st1_ss.at[n, i], st1_rs.at[n, i], s, gp)
    first = [st1(i, src, dst, n) for i in range(4)
             for n, (src, dst) in enumerate(((ck_ref, st1k), (cv_ref, st1v)))]
    for f in first:
        f.start()

    def move(src, dst, ss, rs, sd, mine, gd=gd):
        @pl.when(mine)
        def _():
            pltpu.make_async_copy(src, dst, rs).start()

        @pl.when(jnp.logical_not(mine))
        def _():
            rcopy(src, dst, ss, rs, sd, gd).start()

    has_mine = jnp.logical_and(own, active)

    def sent(piece, n, sem):
        @pl.when(has_mine)
        def _():
            rcopy(piece(n - 1), piece(n - 1), sem, sem, s, sib).wait_send()

        @pl.when(jnp.logical_not(has_mine))
        def _():
            rcopy(piece(n), piece(n), sem, sem, s, sib).wait_send()

    def came(piece, sem):
        rcopy(piece, piece, sem, sem, s, sib).wait_recv()

    def hcols(h):
        return pl.ds(pl.multiple_of(h * HD, HD), HD)

    def krows(slot, n=1):
        return pl.ds(pl.multiple_of(COARSE + slot * TOK, TOK), n * TOK)

    def kv_args(j):
        r, h, sd, mine = dest(j)
        slot = slot_of(j)
        rows = krows(land * 16 + slot)
        return (h, (fk_ref.at[r, :, hcols(h)], kall.at[rows, :], k_ss, k_rs.at[slot >> 2], sd, mine),
                (fv_ref.at[r, :, hcols(h)], vx.at[rows, 0:HD], v_ss, v_rs.at[slot >> 2], sd, mine))

    def q_args(part):
        rows = pl.ds(0, QUART) if part == 0 else pl.ds(QUART, TOK - QUART)

        def args(j):
            r, h, sd, mine = dest(j)
            slot = slot_of(j)
            return h, (q_ref.at[r, rows, hcols(h)], qland.at[slot, rows, :],
                       q_ss.at[part], q_rs.at[part, slot >> 3], sd, mine)
        return args

    def c_args(j):
        r, h, sd, mine = dest(j)
        spot = land * 16 + z * 4 + xl * 2 + (y >> 1)
        rows = pl.ds(pl.multiple_of(spot * 32, 32), 32)
        return (h, (st2k.at[r, :, hcols(h)], kall.at[rows, :], ck_ss, ck_rs, sd, mine),
                (st2v.at[r, :, hcols(h)], vx.at[rows, 0:HD], cv_ss, cv_rs, sd, mine))

    def each(args, what):
        def step(j, carry):
            h, *copies = args(j)

            @pl.when(h < HEADS)
            def _():
                for a in copies:
                    what(*a)
            return carry
        lax.fori_loop(0, 16, step, 0)

    each(kv_args, move)

    for i in range(4):
        for n, (src, dst) in enumerate(((ck_ref, st1k), (cv_ref, st1v))):
            if i == 0:
                st1(0, src, dst, n).wait()
            else:
                st1(i, src, dst, n).wait_recv()
    for r in range(2):
        for a in range(2):
            for src, dst in ((st1k, st2k), (st1v, st2v)):
                lo = src[2 * a].astype(F32)[r * 8:r * 8 + 8]
                hi = src[2 * a + 1].astype(F32)[r * 8:r * 8 + 8]
                dst[r, a * 16:a * 16 + 16, :] = jnp.concatenate([lo, hi], axis=0).astype(BF)
    each(c_args, move)
    each(q_args(0), move)

    ohead = pl.multiple_of(my_h * HD, HD)

    def o_args(ph, j):
        zs, xs, ys = source(j)
        so = zs * 8 + (1 - xs) * 4 + ys
        rows = pl.ds(*PHASES[ph])
        mine = jnp.logical_and(so == s, zk == c)
        return (obuf.at[j, rows, :], att.at[my_r, rows, pl.ds(ohead, HD)], o_ss.at[ph],
                o_rs.at[ph], so, mine, go)

    def give_back(ph, first, count):
        def step(j, carry):
            move(*o_args(ph, j))
            return carry
        lax.fori_loop(first, first + count, step, 0)

    def fwd(ref_k, ss, rs, i, owner, is_v):
        rows = krows(owner * 16 + i * 4, 4)
        piece = ref_k.at[rows, 0:HD] if is_v else ref_k.at[rows, :]
        return rcopy(piece, piece, ss.at[i], rs.at[i], s, sib)

    def cfwd(ref_k, n, owner, is_v):
        rows = pl.ds(pl.multiple_of(owner * 512, 512), 512)
        piece = ref_k.at[rows, 0:HD] if is_v else ref_k.at[rows, :]
        return rcopy(piece, piece, cf_ss.at[n], cf_rs.at[n], s, sib)

    def transpose(row):
        for b in range(2):
            rows = pl.ds(pl.multiple_of(row + b * 256, 256), 256)
            kk = kall[rows, :].T
            kt[0:HD, rows] = kk
            kt[HD:, rows] = kk

    @pl.when(active)
    def _():
        def landed(i, carry):
            rows = krows(c * 16 + i * 4, 4)
            came(kall.at[rows, :], k_rs.at[i])
            fwd(kall, fk_ss, fk_rs, i, c, False).start()
            came(vx.at[rows, 0:HD], v_rs.at[i])
            fwd(vx, fv_ss, fv_rs, i, c, True).start()
            return carry
        lax.fori_loop(0, 4, landed, 0)
        rows = pl.ds(pl.multiple_of(c * 512, 512), 512)
        came(kall.at[rows, :], ck_rs)
        cfwd(kall, 0, c, False).start()
        came(vx.at[rows, 0:HD], cv_rs)
        cfwd(vx, 1, c, True).start()

    sent(lambda n: kall.at[0:n * TOK, :], 14, k_ss)
    sent(lambda n: kall.at[0:n * TOK, :], 14, v_ss)
    each(q_args(1), move)

    scs = (sc0, sc1)

    def prep(quart, half):
        slots = pl.ds(half * 8, 8)

        @pl.when(quart == 0)
        def _():
            came(qland.at[slots, pl.ds(0, QUART), :], q_rs.at[0, half])

        @pl.when(quart == 1)
        def _():
            came(qland.at[slots, pl.ds(QUART, TOK - QUART), :], q_rs.at[1, half])
        rows = pl.ds(pl.multiple_of(quart * QUART, QUART), QUART)
        x = qland[half * 8:half * 8 + 8, rows, :].reshape(TQ, HD).astype(F32) * LOG2
        hi = x.astype(BF)
        qx[:, :HD] = hi
        qx[:, HD:] = (x - hi.astype(F32)).astype(BF)
        mx[...] = jnp.full((TQ, HD), -jnp.inf, F32)

    def qk(cols, sc):
        val = jnp.dot(qx[...], kt[:, cols], preferred_element_type=F32)
        sc[:, cols] = val
        m = mx[...]
        for b in range(CK // HD):
            m = jnp.maximum(m, val[:, b * HD:(b + 1) * HD])
        mx[...] = m

    @pl.when(active)
    def _():
        def mine_t(i, carry):
            transpose(COARSE + c * 2048 + i * 512)
            return carry
        lax.fori_loop(0, 4, mine_t, 0)
        prep(0, 0)

        def early(owner):
            def step(i, carry):
                qk(pl.ds(pl.multiple_of(COARSE + owner * 2048 + i * CK, CK), CK), sc0)
                return carry
            lax.fori_loop(0, 2, step, 0)
        early(c)

        def theirs_t(i, carry):
            fwd(kall, fk_ss, fk_rs, i, 1 - c, False).wait_recv()
            transpose(COARSE + (1 - c) * 2048 + i * 512)
            return carry
        lax.fori_loop(0, 4, theirs_t, 0)
        early(1 - c)

        def theirs_v(i, carry):
            fwd(vx, fv_ss, fv_rs, i, 1 - c, True).wait_recv()
            fwd(kall, fk_ss, fk_rs, i, c, False).wait_send()
            fwd(vx, fv_ss, fv_rs, i, c, True).wait_send()
            return carry
        lax.fori_loop(0, 4, theirs_v, 0)
        cfwd(kall, 0, 1 - c, False).wait_recv()
        cfwd(vx, 1, 1 - c, True).wait_recv()
        cfwd(kall, 0, c, False).wait_send()
        cfwd(vx, 1, c, True).wait_send()

        plen = plen_ref[my_r]
        k0 = kall[COARSE:COARSE + 1, :].astype(F32)
        row = lax.broadcasted_iota(jnp.int32, (256, HD), 0)
        token = 512 + (row >> 6) * 128 + ((row >> 5) & 1) * 64 + (row & 31)
        for i in range(4):
            rows = slice(i * 256, (i + 1) * 256)
            kk = kall[rows, :]
            if i % 2 == 1:
                seen = token + (i // 2) * 32 < plen
                kk = jnp.where(seen, kk.astype(F32), k0).astype(BF)
                vx[rows, 0:HD] = jnp.where(seen, vx[rows, 0:HD].astype(F32), 0.0).astype(BF)
                vx[rows, HD:] = jnp.where(seen, 1.0, 0.0).astype(BF)
            kk = kk.T
            kt[0:HD, rows] = kk
            kt[HD:, rows] = kk
        qk(slice(0, COARSE), sc0)

    def part(ph, gp):
        r0, n = PHASES[ph]
        rows = jnp.concatenate([att[0, r0:r0 + n, :], att[1, r0:r0 + n, :]], axis=0)
        cols = pl.ds(pl.multiple_of(gp * GW, HD), GW)
        return jnp.dot(rows, wv[:, cols], preferred_element_type=F32)

    def pcopy(ph, i):
        rows = pl.ds(2 * PHASES[ph][0], 2 * PHASES[ph][1])
        return rcopy(psend.at[i, rows, :], precv.at[i, rows, :], p_ss.at[ph, i], p_rs.at[ph, i], s, sib)

    def ccopy(ph, i, half):
        rows = pl.ds(*PHASES[ph])
        return rcopy(csend.at[i, :, rows, :], out_ref.at[half, :, rows, :], c_ss.at[ph, i],
                     c_rs.at[ph, half], flip, i * 2 + c)

    def give(ph):
        r0, n = PHASES[ph]

        came(att.at[:, pl.ds(r0, n), :], o_rs.at[ph])
        if ph == 0:
            wcopy.wait()

        def step(i, carry):
            psend[i, 2 * r0:2 * (r0 + n), :] = part(ph, i * 2 + 1 - c).astype(BF)
            pcopy(ph, i).start()
            return carry
        lax.fori_loop(0, 2, step, 0)

    def take(ph):
        r0, n = PHASES[ph]

        def step(i, carry):
            val = part(ph, i * 2 + c)
            pcopy(ph, i).wait_recv()
            val = (val + precv[i, 2 * r0:2 * (r0 + n), :].astype(F32)).astype(BF)
            for r in range(2):
                csend[i, r, r0:r0 + n, :] = val[r * n:(r + 1) * n]
            ccopy(ph, i, xh).start()
            return carry
        lax.fori_loop(0, 2, step, 0)

    def pv(ci, sc, mrow):
        cols = slice(ci * CK, (ci + 1) * CK)
        p = jnp.exp2(sc[:, cols] - mrow).astype(BF)
        acc[...] += jnp.dot(p, vx[cols, :], preferred_element_type=F32)

    def tile(quart, half, final=False):
        mrow = jnp.max(mx[...], axis=1, keepdims=True)
        acc[...] = jnp.zeros((TQ, 2 * HD), F32)
        if not final:
            prep(quart + half, 1 - half)
        for ci in range(KEYS // CK):
            if not final:
                qk(slice(ci * CK, (ci + 1) * CK), scs[1 - half])
            pv(ci, scs[half], mrow)
        o = (acc[:, :HD] / acc[:, HD:]).astype(BF)
        rows = pl.ds(pl.multiple_of(quart * QUART, QUART), QUART)
        obuf[half * 8:half * 8 + 8, rows, :] = o.reshape(8, QUART, HD)

    def quarter(quart, carry):
        @pl.when(active)
        def _():
            tile(quart, 0)

        @pl.when(quart == 2)
        def _():
            give(0)

        @pl.when(active)
        def _():
            tile(quart, 1)

            @pl.when(quart == 0)
            def _():
                give_back(0, 0, 16)

            @pl.when(quart == 2)
            def _():
                give_back(1, 0, 16)
        return carry
    lax.fori_loop(0, 3, quarter, 0)
    take(0)

    @pl.when(active)
    def _():
        tile(3, 0)
        give_back(2, 0, 8)
        tile(3, 1, True)
        give_back(2, 8, 8)
    give(1)
    take(1)
    for i in range(1, 4):
        for n, (src, dst) in enumerate(((ck_ref, st1k), (cv_ref, st1v))):
            st1(i, src, dst, n).wait_send()
    sent(lambda n: kall.at[0:n * 32, :], 14, ck_ss)
    sent(lambda n: kall.at[0:n * 32, :], 14, cv_ss)
    sent(lambda n: qland.at[0:n, pl.ds(0, QUART), :], 14, q_ss.at[0])
    sent(lambda n: qland.at[0:n, pl.ds(QUART, TOK - QUART), :], 14, q_ss.at[1])
    give(2)
    take(2)

    @pl.when(active)
    def _():
        for ph in range(len(PHASES)):
            sent(lambda n: obuf.at[0:n, pl.ds(*PHASES[ph]), :], 16, o_ss.at[ph])
    for ph in range(len(PHASES)):
        for i in range(2):
            pcopy(ph, i).wait_send()
            ccopy(ph, i, xh).wait_send()
    for ph in range(len(PHASES)):
        for i in range(2):
            ccopy(ph, i, i).wait_recv()


def per_device(queries, fine_keys, fine_values, cache_keys, cache_values, prefix_len, out_weight):
    dma = pltpu.SemaphoreType.DMA
    any_spec = pl.BlockSpec(memory_space=pl.ANY)
    halves = pl.pallas_call(
        kernel,
        out_shape=jax.ShapeDtypeStruct((2, 2, TOK, GW), BF),
        in_specs=[any_spec] * 5 + [pl.BlockSpec(memory_space=pltpu.SMEM), any_spec],
        out_specs=any_spec,
        scratch_shapes=[
            pltpu.VMEM((4, 16, GW), BF), pltpu.VMEM((4, 16, GW), BF),
            pltpu.VMEM((2, 32, GW), BF), pltpu.VMEM((2, 32, GW), BF),
            pltpu.VMEM((KEYS, HD), BF), pltpu.VMEM((KEYS, 2 * HD), BF),
            pltpu.VMEM((2 * HD, KEYS), BF), pltpu.VMEM((SLOTS, TOK, HD), BF),
            pltpu.VMEM((TQ, KEYS), F32), pltpu.VMEM((TQ, KEYS), F32),
            pltpu.VMEM((TQ, 2 * HD), BF), pltpu.VMEM((TQ, HD), F32),
            pltpu.VMEM((TQ, 2 * HD), F32), pltpu.VMEM((SLOTS, TOK, HD), BF),
            pltpu.VMEM((2, TOK, GW), BF), pltpu.VMEM((GW, 4 * GW), BF),
            pltpu.VMEM((2, 2 * TOK, GW), BF), pltpu.VMEM((2, 2 * TOK, GW), BF),
            pltpu.VMEM((2, 2, TOK, GW), BF),
            dma((2, 4)), dma((2, 4)), dma, dma((4,)), dma, dma((4,)),
            dma((2,)), dma((2, 2)), dma((4,)), dma((4,)), dma((4,)), dma((4,)),
            dma, dma, dma, dma, dma((2,)), dma((2,)),
            dma((3,)), dma((3,)), dma((3, 2)), dma((3, 2)), dma((3, 2)), dma((3, 2)), dma,
        ],
        compiler_params=pltpu.CompilerParams(
            collective_id=0, has_side_effects=True, vmem_limit_bytes=58 * 2**20),
        cost_estimate=pl.CostEstimate(flops=7_000_000_000, bytes_accessed=12_000_000, transcendentals=10_000_000),
    )(queries, fine_keys, fine_values, cache_keys.reshape(16, 4 * GW),
      cache_values.reshape(16, 4 * GW), prefix_len, out_weight)
    return (halves[0].astype(F32) + halves[1].astype(F32)).astype(BF)


def solution(mesh):
    return jax.shard_map(
        per_device,
        mesh=mesh,
        in_specs=(
            P(None, "seq", "head"),
            P(None, "seq", "head"),
            P(None, "seq", "head"),
            P(None, ("seq", "head"), None),
            P(None, ("seq", "head"), None),
            P(),
            P("head", None),
        ),
        out_specs=P(None, "seq", "head"),
        check_vma=False,
    )
```

```python
import functools

import jax
import jax.numpy as jnp
from jax import lax
from jax.experimental import pallas as pl
from jax.experimental.pallas import tpu as pltpu
from jax.sharding import PartitionSpec as P

MESH = pl.DeviceIdType.MESH
F32, BF = jnp.float32, jnp.bfloat16
HD = 128
HEADS = 7
GW = HEADS * HD
TOK = 128
COARSE = 1024
KEYS = 5120
TQ = 256
CK = 1024
SLOTS = 16
QUART = TOK // 4
PARTS = ((0, 32), (32, 32), (64, 64))
PHASES = ((0, 32), (32, 64), (96, 32))
LOG2 = float(HD ** -0.5 * 1.4426950408889634)


def rcopy(src, dst, ssem, rsem, s, g):
    return pltpu.make_async_remote_copy(
        src_ref=src, dst_ref=dst, send_sem=ssem, recv_sem=rsem,
        device_id=(s, g), device_id_type=MESH)


def kernel(q_ref, fk_ref, fv_ref, ck_ref, cv_ref, plen_ref, w_ref, out_ref,
           st1k, st1v, st2k, st2v, kall, vx, kt, qland, sc0, sc1, qx, mx, acc, obuf, att, wv,
           psend, precv, csend,
           st1_ss, st1_rs, k_ss, k_rs, v_ss, v_rs, q_ss, q_rs, fk_ss, fk_rs, fv_ss, fv_rs,
           ck_ss, ck_rs, cv_ss, cv_rs, cf_ss, cf_rs, o_ss, o_rs, p_ss, p_rs, c_ss, c_rs, w_sem):
    s = lax.axis_index("seq")
    g = lax.axis_index("head")
    z, xl, y = s >> 3, (s >> 2) & 1, s & 3
    xh, c = g >> 1, g & 1
    zk = z >> 1
    land = y & 1
    sib = xh * 2 + 1 - c
    flip = z * 8 + (1 - xl) * 4 + y

    def place(zd, pos):
        return (pos + 8 - 2 * zd) & 7

    def dest(j):
        zb, xb, yb = j >> 3, (j >> 2) & 1, j & 3
        r = (z + zb) & 1
        zd = 2 * c + r
        pos = ((xl + xb) & 1) * 4 + ((y + yb) & 3)
        h = place(zd, pos)
        sd = zd * 8 + pos
        mine = jnp.logical_and(sd == s, land == c)
        return r, h, sd, mine

    my_r = z & 1
    my_h = place(z, xl * 4 + y)
    active = my_h < HEADS

    def slot_of(j):
        return (z >> 1) * 8 + (j >> 3) * 4 + ((j >> 2) & 1) * 2 + ((j & 3) >> 1)

    def source(slot):
        zs = (slot >> 3) * 2 + ((my_r + (slot >> 2)) & 1)
        yb = (slot & 1) * 2 + ((y + c) & 1)
        return zs, (xl + (slot >> 1)) & 1, (y + 4 - yb) & 3

    barrier = pltpu.get_barrier_semaphore()
    gd = xh * 2 + land
    go = xh * 2 + zk

    def greet(j, carry):
        _, _, sd, mine = dest(j)
        zs, xs, ys = source(j)
        ss = zs * 8 + xs * 4 + ys

        @pl.when(jnp.logical_not(mine))
        def _():
            pl.semaphore_signal(barrier, inc=1, device_id=(sd, gd), device_id_type=MESH)

        @pl.when(jnp.logical_not(jnp.logical_and(ss == s, zk == c)))
        def _():
            pl.semaphore_signal(barrier, inc=1, device_id=(ss, go), device_id_type=MESH)
        return carry
    lax.fori_loop(0, 16, greet, 0)
    own = jnp.logical_and(zk == c, land == c)
    for i in range(1, 4):
        pl.semaphore_signal(barrier, inc=1, device_id=(s, (g + i) & 3), device_id_type=MESH)
    for i in range(2):
        pl.semaphore_signal(barrier, inc=1, device_id=(flip, i * 2 + c), device_id_type=MESH)
    wcopy = pltpu.make_async_copy(w_ref, wv, w_sem)
    wcopy.start()
    vx[:, HD:] = jnp.ones((KEYS, HD), BF)
    pl.semaphore_wait(barrier, 37 - jnp.where(own, 2, 0))


    def st1(i, src, dst, n):
        gp = (g + i) & 3
        cols = pl.ds(pl.multiple_of(gp * GW, HD), GW)
        if i == 0:
            return pltpu.make_async_copy(src.at[:, cols], dst.at[g], st1_rs.at[n, 0])
        return rcopy(src.at[:, cols], dst.at[g], st1_ss.at[n, i], st1_rs.at[n, i], s, gp)
    first = [st1(i, src, dst, n) for i in range(4)
             for n, (src, dst) in enumerate(((ck_ref, st1k), (cv_ref, st1v)))]
    for f in first:
        f.start()

    def move(src, dst, ss, rs, sd, mine, gd=gd):
        @pl.when(mine)
        def _():
            pltpu.make_async_copy(src, dst, rs).start()

        @pl.when(jnp.logical_not(mine))
        def _():
            rcopy(src, dst, ss, rs, sd, gd).start()

    has_mine = jnp.logical_and(own, active)

    def sent(piece, n, sem):
        @pl.when(has_mine)
        def _():
            rcopy(piece(n - 1), piece(n - 1), sem, sem, s, sib).wait_send()

        @pl.when(jnp.logical_not(has_mine))
        def _():
            rcopy(piece(n), piece(n), sem, sem, s, sib).wait_send()

    def came(piece, sem):
        rcopy(piece, piece, sem, sem, s, sib).wait_recv()

    def hcols(h):
        return pl.ds(pl.multiple_of(h * HD, HD), HD)

    def krows(slot, n=1):
        return pl.ds(pl.multiple_of(COARSE + slot * TOK, TOK), n * TOK)

    def kv_args(j):
        r, h, sd, mine = dest(j)
        slot = slot_of(j)
        rows = krows(land * 16 + slot)
        return (h, (fk_ref.at[r, :, hcols(h)], kall.at[rows, :], k_ss, k_rs.at[slot >> 2], sd, mine),
                (fv_ref.at[r, :, hcols(h)], vx.at[rows, 0:HD], v_ss, v_rs.at[slot >> 2], sd, mine))

    def q_args(part):
        rows = pl.ds(*PARTS[part])

        def args(j):
            r, h, sd, mine = dest(j)
            slot = slot_of(j)
            return h, (q_ref.at[r, rows, hcols(h)], qland.at[slot, rows, :],
                       q_ss.at[part], q_rs.at[part, slot >> 3], sd, mine)
        return args

    def c_args(j):
        r, h, sd, mine = dest(j)
        spot = land * 16 + z * 4 + xl * 2 + (y >> 1)
        rows = pl.ds(pl.multiple_of(spot * 32, 32), 32)
        return (h, (st2k.at[r, :, hcols(h)], kall.at[rows, :], ck_ss, ck_rs, sd, mine),
                (st2v.at[r, :, hcols(h)], vx.at[rows, 0:HD], cv_ss, cv_rs, sd, mine))

    def each(args, what):
        def step(j, carry):
            h, *copies = args(j)

            @pl.when(h < HEADS)
            def _():
                for a in copies:
                    what(*a)
            return carry
        lax.fori_loop(0, 16, step, 0)

    each(kv_args, move)

    for i in range(4):
        for n, (src, dst) in enumerate(((ck_ref, st1k), (cv_ref, st1v))):
            if i == 0:
                st1(0, src, dst, n).wait()
            else:
                st1(i, src, dst, n).wait_recv()
    for r in range(2):
        for a in range(2):
            for src, dst in ((st1k, st2k), (st1v, st2v)):
                lo = src[2 * a].astype(F32)[r * 8:r * 8 + 8]
                hi = src[2 * a + 1].astype(F32)[r * 8:r * 8 + 8]
                dst[r, a * 16:a * 16 + 16, :] = jnp.concatenate([lo, hi], axis=0).astype(BF)
    each(c_args, move)
    each(q_args(0), move)

    ohead = pl.multiple_of(my_h * HD, HD)

    def o_args(ph, j):
        zs, xs, ys = source(j)
        so = zs * 8 + (1 - xs) * 4 + ys
        rows = pl.ds(*PHASES[ph])
        mine = jnp.logical_and(so == s, zk == c)
        return (obuf.at[j, rows, :], att.at[my_r, rows, pl.ds(ohead, HD)], o_ss.at[ph],
                o_rs.at[ph], so, mine, go)

    def give_back(ph, first, count):
        def step(j, carry):
            move(*o_args(ph, j))
            return carry
        lax.fori_loop(first, first + count, step, 0)

    def fwd(ref_k, ss, rs, i, owner, is_v):
        rows = krows(owner * 16 + i * 4, 4)
        piece = ref_k.at[rows, 0:HD] if is_v else ref_k.at[rows, :]
        return rcopy(piece, piece, ss.at[i], rs.at[i], s, sib)

    def cfwd(ref_k, n, owner, is_v):
        rows = pl.ds(pl.multiple_of(owner * 512, 512), 512)
        piece = ref_k.at[rows, 0:HD] if is_v else ref_k.at[rows, :]
        return rcopy(piece, piece, cf_ss.at[n], cf_rs.at[n], s, sib)

    def transpose(row):
        for b in range(2):
            rows = pl.ds(pl.multiple_of(row + b * 256, 256), 256)
            kk = kall[rows, :].T
            kt[0:HD, rows] = kk
            kt[HD:, rows] = kk

    @pl.when(active)
    def _():
        def landed(i, carry):
            rows = krows(c * 16 + i * 4, 4)
            came(kall.at[rows, :], k_rs.at[i])
            fwd(kall, fk_ss, fk_rs, i, c, False).start()
            came(vx.at[rows, 0:HD], v_rs.at[i])
            fwd(vx, fv_ss, fv_rs, i, c, True).start()
            return carry
        lax.fori_loop(0, 4, landed, 0)
        rows = pl.ds(pl.multiple_of(c * 512, 512), 512)
        came(kall.at[rows, :], ck_rs)
        cfwd(kall, 0, c, False).start()
        came(vx.at[rows, 0:HD], cv_rs)
        cfwd(vx, 1, c, True).start()

    sent(lambda n: kall.at[0:n * TOK, :], 14, k_ss)
    sent(lambda n: kall.at[0:n * TOK, :], 14, v_ss)
    each(q_args(1), move)
    each(q_args(2), move)

    scs = (sc0, sc1)

    def prep(quart, half):
        slots = pl.ds(half * 8, 8)

        for b in range(len(PARTS)):
            @pl.when(quart == PARTS[b][0] // QUART)
            def _():
                came(qland.at[slots, pl.ds(*PARTS[b]), :], q_rs.at[b, half])
        rows = pl.ds(pl.multiple_of(quart * QUART, QUART), QUART)
        x = qland[half * 8:half * 8 + 8, rows, :].reshape(TQ, HD).astype(F32) * LOG2
        hi = x.astype(BF)
        qx[:, :HD] = hi
        qx[:, HD:] = (x - hi.astype(F32)).astype(BF)
        mx[...] = jnp.full((TQ, HD), -jnp.inf, F32)

    def qk(cols, sc):
        val = jnp.dot(qx[...], kt[:, cols], preferred_element_type=F32)
        sc[:, cols] = val
        m = mx[...]
        for b in range(CK // HD):
            m = jnp.maximum(m, val[:, b * HD:(b + 1) * HD])
        mx[...] = m

    @pl.when(active)
    def _():
        def mine_t(i, carry):
            transpose(COARSE + c * 2048 + i * 512)
            return carry
        lax.fori_loop(0, 4, mine_t, 0)
        prep(0, 0)

        def early(owner):
            def step(i, carry):
                qk(pl.ds(pl.multiple_of(COARSE + owner * 2048 + i * CK, CK), CK), sc0)
                return carry
            lax.fori_loop(0, 2, step, 0)
        early(c)

        def theirs_t(i, carry):
            fwd(kall, fk_ss, fk_rs, i, 1 - c, False).wait_recv()
            transpose(COARSE + (1 - c) * 2048 + i * 512)
            return carry
        lax.fori_loop(0, 4, theirs_t, 0)
        early(1 - c)

        def theirs_v(i, carry):
            fwd(vx, fv_ss, fv_rs, i, 1 - c, True).wait_recv()
            fwd(kall, fk_ss, fk_rs, i, c, False).wait_send()
            fwd(vx, fv_ss, fv_rs, i, c, True).wait_send()
            return carry
        lax.fori_loop(0, 4, theirs_v, 0)
        cfwd(kall, 0, 1 - c, False).wait_recv()
        cfwd(vx, 1, 1 - c, True).wait_recv()
        cfwd(kall, 0, c, False).wait_send()
        cfwd(vx, 1, c, True).wait_send()

        plen = plen_ref[my_r]
        k0 = kall[COARSE:COARSE + 1, :].astype(F32)
        row = lax.broadcasted_iota(jnp.int32, (256, HD), 0)
        token = 512 + (row >> 6) * 128 + ((row >> 5) & 1) * 64 + (row & 31)
        for i in range(4):
            rows = slice(i * 256, (i + 1) * 256)
            kk = kall[rows, :]
            if i % 2 == 1:
                seen = token + (i // 2) * 32 < plen
                kk = jnp.where(seen, kk.astype(F32), k0).astype(BF)
                vx[rows, 0:HD] = jnp.where(seen, vx[rows, 0:HD].astype(F32), 0.0).astype(BF)
                vx[rows, HD:] = jnp.where(seen, 1.0, 0.0).astype(BF)
            kk = kk.T
            kt[0:HD, rows] = kk
            kt[HD:, rows] = kk
        qk(slice(0, COARSE), sc0)

    def part(ph, gp):
        r0, n = PHASES[ph]
        rows = jnp.concatenate([att[0, r0:r0 + n, :], att[1, r0:r0 + n, :]], axis=0)
        cols = pl.ds(pl.multiple_of(gp * GW, HD), GW)
        return jnp.dot(rows, wv[:, cols], preferred_element_type=F32)

    def pcopy(ph, i):
        rows = pl.ds(2 * PHASES[ph][0], 2 * PHASES[ph][1])
        return rcopy(psend.at[i, rows, :], precv.at[i, rows, :], p_ss.at[ph, i], p_rs.at[ph, i], s, sib)

    def ccopy(ph, i, half):
        rows = pl.ds(*PHASES[ph])
        return rcopy(csend.at[i, :, rows, :], out_ref.at[half, :, rows, :], c_ss.at[ph, i],
                     c_rs.at[ph, half], flip, i * 2 + c)

    def give(ph):
        r0, n = PHASES[ph]

        came(att.at[:, pl.ds(r0, n), :], o_rs.at[ph])
        if ph == 0:
            wcopy.wait()

        def step(i, carry):
            psend[i, 2 * r0:2 * (r0 + n), :] = part(ph, i * 2 + 1 - c).astype(BF)
            pcopy(ph, i).start()
            return carry
        lax.fori_loop(0, 2, step, 0)

    def take(ph):
        r0, n = PHASES[ph]

        def step(i, carry):
            val = part(ph, i * 2 + c)
            pcopy(ph, i).wait_recv()
            val = (val + precv[i, 2 * r0:2 * (r0 + n), :].astype(F32)).astype(BF)
            for r in range(2):
                csend[i, r, r0:r0 + n, :] = val[r * n:(r + 1) * n]
            ccopy(ph, i, xh).start()
            return carry
        lax.fori_loop(0, 2, step, 0)

    def pv(ci, sc, mrow):
        cols = slice(ci * CK, (ci + 1) * CK)
        p = jnp.exp2(sc[:, cols] - mrow).astype(BF)
        acc[...] += jnp.dot(p, vx[cols, :], preferred_element_type=F32)

    def tile(quart, half, final=False):
        mrow = jnp.max(mx[...], axis=1, keepdims=True)
        acc[...] = jnp.zeros((TQ, 2 * HD), F32)
        if not final:
            prep(quart + half, 1 - half)
        for ci in range(KEYS // CK):
            if not final:
                qk(slice(ci * CK, (ci + 1) * CK), scs[1 - half])
            pv(ci, scs[half], mrow)
        o = (acc[:, :HD] / acc[:, HD:]).astype(BF)
        rows = pl.ds(pl.multiple_of(quart * QUART, QUART), QUART)
        obuf[half * 8:half * 8 + 8, rows, :] = o.reshape(8, QUART, HD)

    def quarter(quart, carry):
        @pl.when(active)
        def _():
            tile(quart, 0)

        @pl.when(quart == 2)
        def _():
            give(0)

        @pl.when(active)
        def _():
            tile(quart, 1)

            @pl.when(quart == 0)
            def _():
                give_back(0, 0, 16)

            @pl.when(quart == 2)
            def _():
                give_back(1, 0, 16)
        return carry
    lax.fori_loop(0, 3, quarter, 0)
    take(0)

    @pl.when(active)
    def _():
        tile(3, 0)
        give_back(2, 0, 8)
        tile(3, 1, True)
        give_back(2, 8, 8)
    give(1)
    take(1)
    for i in range(1, 4):
        for n, (src, dst) in enumerate(((ck_ref, st1k), (cv_ref, st1v))):
            st1(i, src, dst, n).wait_send()
    sent(lambda n: kall.at[0:n * 32, :], 14, ck_ss)
    sent(lambda n: kall.at[0:n * 32, :], 14, cv_ss)
    for b in range(len(PARTS)):
        sent(lambda n: qland.at[0:n, pl.ds(*PARTS[b]), :], 14, q_ss.at[b])
    give(2)
    take(2)

    @pl.when(active)
    def _():
        for ph in range(len(PHASES)):
            sent(lambda n: obuf.at[0:n, pl.ds(*PHASES[ph]), :], 16, o_ss.at[ph])
    for ph in range(len(PHASES)):
        for i in range(2):
            pcopy(ph, i).wait_send()
            ccopy(ph, i, xh).wait_send()
    for ph in range(len(PHASES)):
        for i in range(2):
            ccopy(ph, i, i).wait_recv()


def per_device(queries, fine_keys, fine_values, cache_keys, cache_values, prefix_len, out_weight):
    dma = pltpu.SemaphoreType.DMA
    any_spec = pl.BlockSpec(memory_space=pl.ANY)
    halves = pl.pallas_call(
        kernel,
        out_shape=jax.ShapeDtypeStruct((2, 2, TOK, GW), BF),
        in_specs=[any_spec] * 5 + [pl.BlockSpec(memory_space=pltpu.SMEM), any_spec],
        out_specs=any_spec,
        scratch_shapes=[
            pltpu.VMEM((4, 16, GW), BF), pltpu.VMEM((4, 16, GW), BF),
            pltpu.VMEM((2, 32, GW), BF), pltpu.VMEM((2, 32, GW), BF),
            pltpu.VMEM((KEYS, HD), BF), pltpu.VMEM((KEYS, 2 * HD), BF),
            pltpu.VMEM((2 * HD, KEYS), BF), pltpu.VMEM((SLOTS, TOK, HD), BF),
            pltpu.VMEM((TQ, KEYS), F32), pltpu.VMEM((TQ, KEYS), F32),
            pltpu.VMEM((TQ, 2 * HD), BF), pltpu.VMEM((TQ, HD), F32),
            pltpu.VMEM((TQ, 2 * HD), F32), pltpu.VMEM((SLOTS, TOK, HD), BF),
            pltpu.VMEM((2, TOK, GW), BF), pltpu.VMEM((GW, 4 * GW), BF),
            pltpu.VMEM((2, 2 * TOK, GW), BF), pltpu.VMEM((2, 2 * TOK, GW), BF),
            pltpu.VMEM((2, 2, TOK, GW), BF),
            dma((2, 4)), dma((2, 4)), dma, dma((4,)), dma, dma((4,)),
            dma((3,)), dma((3, 2)), dma((4,)), dma((4,)), dma((4,)), dma((4,)),
            dma, dma, dma, dma, dma((2,)), dma((2,)),
            dma((3,)), dma((3,)), dma((3, 2)), dma((3, 2)), dma((3, 2)), dma((3, 2)), dma,
        ],
        compiler_params=pltpu.CompilerParams(
            collective_id=0, has_side_effects=True, vmem_limit_bytes=58 * 2**20),
        cost_estimate=pl.CostEstimate(flops=7_000_000_000, bytes_accessed=12_000_000, transcendentals=10_000_000),
    )(queries, fine_keys, fine_values, cache_keys.reshape(16, 4 * GW),
      cache_values.reshape(16, 4 * GW), prefix_len, out_weight)
    return (halves[0].astype(F32) + halves[1].astype(F32)).astype(BF)


def solution(mesh):
    return jax.shard_map(
        per_device,
        mesh=mesh,
        in_specs=(
            P(None, "seq", "head"),
            P(None, "seq", "head"),
            P(None, "seq", "head"),
            P(None, ("seq", "head"), None),
            P(None, ("seq", "head"), None),
            P(),
            P("head", None),
        ),
        out_specs=P(None, "seq", "head"),
        check_vma=False,
    )
```

```python
import functools

import jax
import jax.numpy as jnp
from jax import lax
from jax.experimental import pallas as pl
from jax.experimental.pallas import tpu as pltpu
from jax.sharding import PartitionSpec as P

MESH = pl.DeviceIdType.MESH
F32, BF = jnp.float32, jnp.bfloat16
HD = 128
HEADS = 7
GW = HEADS * HD
TOK = 128
COARSE = 1024
KEYS = 5120
TQ = 256
CK = 1024
SLOTS = 16
QUART = TOK // 4
PARTS = ((0, 32), (32, 32), (64, 64))
PHASES = ((0, 32), (32, 64), (96, 32))
LOG2 = float(HD ** -0.5 * 1.4426950408889634)


def rcopy(src, dst, ssem, rsem, s, g):
    return pltpu.make_async_remote_copy(
        src_ref=src, dst_ref=dst, send_sem=ssem, recv_sem=rsem,
        device_id=(s, g), device_id_type=MESH)


def kernel(q_ref, fk_ref, fv_ref, ck_ref, cv_ref, plen_ref, w_ref, out_ref,
           st1k, st1v, st2k, st2v, kall, vx, kt, qland, sc0, sc1, qx, mx, acc, obuf, att, wv,
           psend, precv, csend,
           st1_ss, st1_rs, k_ss, k_rs, v_ss, v_rs, q_ss, q_rs, fk_ss, fk_rs, fv_ss, fv_rs,
           ck_ss, ck_rs, cv_ss, cv_rs, cf_ss, cf_rs, o_ss, o_rs, p_ss, p_rs, c_ss, c_rs, w_sem):
    s = lax.axis_index("seq")
    g = lax.axis_index("head")
    z, xl, y = s >> 3, (s >> 2) & 1, s & 3
    xh, c = g >> 1, g & 1
    zk = z >> 1
    land = y & 1
    sib = xh * 2 + 1 - c
    flip = z * 8 + (1 - xl) * 4 + y

    def place(zd, pos):
        return (pos + 8 - 2 * zd) & 7

    def dest(j):
        zb, xb, yb = j >> 3, (j >> 2) & 1, j & 3
        r = (z + zb) & 1
        zd = 2 * c + r
        pos = ((xl + xb) & 1) * 4 + ((y + yb) & 3)
        h = place(zd, pos)
        sd = zd * 8 + pos
        mine = jnp.logical_and(sd == s, land == c)
        return r, h, sd, mine

    my_r = z & 1
    my_h = place(z, xl * 4 + y)
    active = my_h < HEADS

    def slot_of(j):
        return (z >> 1) * 8 + (j >> 3) * 4 + ((j >> 2) & 1) * 2 + ((j & 3) >> 1)

    def source(slot):
        zs = (slot >> 3) * 2 + ((my_r + (slot >> 2)) & 1)
        yb = (slot & 1) * 2 + ((y + c) & 1)
        return zs, (xl + (slot >> 1)) & 1, (y + 4 - yb) & 3

    barrier = pltpu.get_barrier_semaphore()
    gd = xh * 2 + land
    go = xh * 2 + zk

    def greet(sp, gp, maybe_here):
        def signal():
            pl.semaphore_signal(barrier, inc=1, device_id=(sp, gp), device_id_type=MESH)
        if maybe_here:
            pl.when(jnp.logical_not(jnp.logical_and(sp == s, gp == g)))(signal)
        else:
            signal()
    for j in range(15, -1, -1):
        greet(dest(j)[2], gd, j & 7 == 0)
        zs, xs, ys = source(j)
        greet(zs * 8 + xs * 4 + ys, go, j & 3 == 0)
    own = jnp.logical_and(zk == c, land == c)
    for i in range(1, 4):
        pl.semaphore_signal(barrier, inc=1, device_id=(s, (g + i) & 3), device_id_type=MESH)
    for i in range(2):
        pl.semaphore_signal(barrier, inc=1, device_id=(flip, i * 2 + c), device_id_type=MESH)
    wcopy = pltpu.make_async_copy(w_ref, wv, w_sem)
    wcopy.start()
    vx[:, HD:] = jnp.ones((KEYS, HD), BF)
    pl.semaphore_wait(barrier, 37 - jnp.where(own, 2, 0))


    def st1(i, src, dst, n):
        gp = (g + i) & 3
        cols = pl.ds(pl.multiple_of(gp * GW, HD), GW)
        if i == 0:
            return pltpu.make_async_copy(src.at[:, cols], dst.at[g], st1_rs.at[n, 0])
        return rcopy(src.at[:, cols], dst.at[g], st1_ss.at[n, i], st1_rs.at[n, i], s, gp)
    first = [st1(i, src, dst, n) for i in range(4)
             for n, (src, dst) in enumerate(((ck_ref, st1k), (cv_ref, st1v)))]
    for f in first:
        f.start()

    def move(src, dst, ss, rs, sd, mine, gd=gd):
        @pl.when(mine)
        def _():
            pltpu.make_async_copy(src, dst, rs).start()

        @pl.when(jnp.logical_not(mine))
        def _():
            rcopy(src, dst, ss, rs, sd, gd).start()

    has_mine = jnp.logical_and(own, active)

    def sent(piece, n, sem):
        @pl.when(has_mine)
        def _():
            rcopy(piece(n - 1), piece(n - 1), sem, sem, s, sib).wait_send()

        @pl.when(jnp.logical_not(has_mine))
        def _():
            rcopy(piece(n), piece(n), sem, sem, s, sib).wait_send()

    def came(piece, sem):
        rcopy(piece, piece, sem, sem, s, sib).wait_recv()

    def hcols(h):
        return pl.ds(pl.multiple_of(h * HD, HD), HD)

    def krows(slot, n=1):
        return pl.ds(pl.multiple_of(COARSE + slot * TOK, TOK), n * TOK)

    def kv_args(j):
        r, h, sd, mine = dest(j)
        slot = slot_of(j)
        rows = krows(land * 16 + slot)
        return (h, (fk_ref.at[r, :, hcols(h)], kall.at[rows, :], k_ss, k_rs.at[slot >> 2], sd, mine),
                (fv_ref.at[r, :, hcols(h)], vx.at[rows, 0:HD], v_ss, v_rs.at[slot >> 2], sd, mine))

    def q_args(part):
        rows = pl.ds(*PARTS[part])

        def args(j):
            r, h, sd, mine = dest(j)
            slot = slot_of(j)
            return h, (q_ref.at[r, rows, hcols(h)], qland.at[slot, rows, :],
                       q_ss.at[part], q_rs.at[part, slot >> 3], sd, mine)
        return args

    def c_args(j):
        r, h, sd, mine = dest(j)
        spot = land * 16 + z * 4 + xl * 2 + (y >> 1)
        rows = pl.ds(pl.multiple_of(spot * 32, 32), 32)
        return (h, (st2k.at[r, :, hcols(h)], kall.at[rows, :], ck_ss, ck_rs, sd, mine),
                (st2v.at[r, :, hcols(h)], vx.at[rows, 0:HD], cv_ss, cv_rs, sd, mine))

    def each(args, what):
        def step(j, carry):
            h, *copies = args(j)

            @pl.when(h < HEADS)
            def _():
                for a in copies:
                    what(*a)
            return carry
        lax.fori_loop(0, 16, step, 0)

    each(kv_args, move)

    for i in range(4):
        for n, (src, dst) in enumerate(((ck_ref, st1k), (cv_ref, st1v))):
            if i == 0:
                st1(0, src, dst, n).wait()
            else:
                st1(i, src, dst, n).wait_recv()
    for r in range(2):
        for a in range(2):
            for src, dst in ((st1k, st2k), (st1v, st2v)):
                lo = src[2 * a].astype(F32)[r * 8:r * 8 + 8]
                hi = src[2 * a + 1].astype(F32)[r * 8:r * 8 + 8]
                dst[r, a * 16:a * 16 + 16, :] = jnp.concatenate([lo, hi], axis=0).astype(BF)
    each(c_args, move)
    each(q_args(0), move)

    ohead = pl.multiple_of(my_h * HD, HD)

    def o_args(ph, j):
        zs, xs, ys = source(j)
        so = zs * 8 + (1 - xs) * 4 + ys
        rows = pl.ds(*PHASES[ph])
        mine = jnp.logical_and(so == s, zk == c)
        return (obuf.at[j, rows, :], att.at[my_r, rows, pl.ds(ohead, HD)], o_ss.at[ph],
                o_rs.at[ph], so, mine, go)

    def give_back(ph, first, count):
        def step(j, carry):
            move(*o_args(ph, j))
            return carry
        lax.fori_loop(first, first + count, step, 0)

    def fwd(ref_k, ss, rs, i, owner, is_v):
        rows = krows(owner * 16 + i * 4, 4)
        piece = ref_k.at[rows, 0:HD] if is_v else ref_k.at[rows, :]
        return rcopy(piece, piece, ss.at[i], rs.at[i], s, sib)

    def cfwd(ref_k, n, owner, is_v):
        rows = pl.ds(pl.multiple_of(owner * 512, 512), 512)
        piece = ref_k.at[rows, 0:HD] if is_v else ref_k.at[rows, :]
        return rcopy(piece, piece, cf_ss.at[n], cf_rs.at[n], s, sib)

    def transpose(row):
        for b in range(2):
            rows = pl.ds(pl.multiple_of(row + b * 256, 256), 256)
            kk = kall[rows, :].T
            kt[0:HD, rows] = kk
            kt[HD:, rows] = kk

    @pl.when(active)
    def _():
        def landed(i, carry):
            rows = krows(c * 16 + i * 4, 4)
            came(kall.at[rows, :], k_rs.at[i])
            fwd(kall, fk_ss, fk_rs, i, c, False).start()
            came(vx.at[rows, 0:HD], v_rs.at[i])
            fwd(vx, fv_ss, fv_rs, i, c, True).start()
            return carry
        lax.fori_loop(0, 4, landed, 0)
        rows = pl.ds(pl.multiple_of(c * 512, 512), 512)
        came(kall.at[rows, :], ck_rs)
        cfwd(kall, 0, c, False).start()
        came(vx.at[rows, 0:HD], cv_rs)
        cfwd(vx, 1, c, True).start()

    sent(lambda n: kall.at[0:n * TOK, :], 14, k_ss)
    sent(lambda n: kall.at[0:n * TOK, :], 14, v_ss)
    each(q_args(1), move)
    each(q_args(2), move)

    scs = (sc0, sc1)

    def prep(quart, half):
        slots = pl.ds(half * 8, 8)

        for b in range(len(PARTS)):
            @pl.when(quart == PARTS[b][0] // QUART)
            def _():
                came(qland.at[slots, pl.ds(*PARTS[b]), :], q_rs.at[b, half])
        rows = pl.ds(pl.multiple_of(quart * QUART, QUART), QUART)
        x = qland[half * 8:half * 8 + 8, rows, :].reshape(TQ, HD).astype(F32) * LOG2
        hi = x.astype(BF)
        qx[:, :HD] = hi
        qx[:, HD:] = (x - hi.astype(F32)).astype(BF)
        mx[...] = jnp.full((TQ, HD), -jnp.inf, F32)

    def qk(cols, sc):
        val = jnp.dot(qx[...], kt[:, cols], preferred_element_type=F32)
        sc[:, cols] = val
        m = mx[...]
        for b in range(CK // HD):
            m = jnp.maximum(m, val[:, b * HD:(b + 1) * HD])
        mx[...] = m

    @pl.when(active)
    def _():
        def mine_t(i, carry):
            transpose(COARSE + c * 2048 + i * 512)
            return carry
        lax.fori_loop(0, 4, mine_t, 0)
        prep(0, 0)

        def early(owner):
            def step(i, carry):
                qk(pl.ds(pl.multiple_of(COARSE + owner * 2048 + i * CK, CK), CK), sc0)
                return carry
            lax.fori_loop(0, 2, step, 0)
        early(c)

        def theirs_t(i, carry):
            fwd(kall, fk_ss, fk_rs, i, 1 - c, False).wait_recv()
            transpose(COARSE + (1 - c) * 2048 + i * 512)
            return carry
        lax.fori_loop(0, 4, theirs_t, 0)
        early(1 - c)

        def theirs_v(i, carry):
            fwd(vx, fv_ss, fv_rs, i, 1 - c, True).wait_recv()
            fwd(kall, fk_ss, fk_rs, i, c, False).wait_send()
            fwd(vx, fv_ss, fv_rs, i, c, True).wait_send()
            return carry
        lax.fori_loop(0, 4, theirs_v, 0)
        cfwd(kall, 0, 1 - c, False).wait_recv()
        cfwd(vx, 1, 1 - c, True).wait_recv()
        cfwd(kall, 0, c, False).wait_send()
        cfwd(vx, 1, c, True).wait_send()

        plen = plen_ref[my_r]
        k0 = kall[COARSE:COARSE + 1, :].astype(F32)
        row = lax.broadcasted_iota(jnp.int32, (256, HD), 0)
        token = 512 + (row >> 6) * 128 + ((row >> 5) & 1) * 64 + (row & 31)
        for i in range(4):
            rows = slice(i * 256, (i + 1) * 256)
            kk = kall[rows, :]
            if i % 2 == 1:
                seen = token + (i // 2) * 32 < plen
                kk = jnp.where(seen, kk.astype(F32), k0).astype(BF)
                vx[rows, 0:HD] = jnp.where(seen, vx[rows, 0:HD].astype(F32), 0.0).astype(BF)
                vx[rows, HD:] = jnp.where(seen, 1.0, 0.0).astype(BF)
            kk = kk.T
            kt[0:HD, rows] = kk
            kt[HD:, rows] = kk
        qk(slice(0, COARSE), sc0)

    def part(ph, gp):
        r0, n = PHASES[ph]
        rows = jnp.concatenate([att[0, r0:r0 + n, :], att[1, r0:r0 + n, :]], axis=0)
        cols = pl.ds(pl.multiple_of(gp * GW, HD), GW)
        return jnp.dot(rows, wv[:, cols], preferred_element_type=F32)

    def pcopy(ph, i):
        rows = pl.ds(2 * PHASES[ph][0], 2 * PHASES[ph][1])
        return rcopy(psend.at[i, rows, :], precv.at[i, rows, :], p_ss.at[ph, i], p_rs.at[ph, i], s, sib)

    def ccopy(ph, i, half):
        rows = pl.ds(*PHASES[ph])
        return rcopy(csend.at[i, :, rows, :], out_ref.at[half, :, rows, :], c_ss.at[ph, i],
                     c_rs.at[ph, half], flip, i * 2 + c)

    def give(ph):
        r0, n = PHASES[ph]

        came(att.at[:, pl.ds(r0, n), :], o_rs.at[ph])
        if ph == 0:
            wcopy.wait()

        def step(i, carry):
            psend[i, 2 * r0:2 * (r0 + n), :] = part(ph, i * 2 + 1 - c).astype(BF)
            pcopy(ph, i).start()
            return carry
        lax.fori_loop(0, 2, step, 0)

    def take(ph):
        r0, n = PHASES[ph]

        def step(i, carry):
            val = part(ph, i * 2 + c)
            pcopy(ph, i).wait_recv()
            val = (val + precv[i, 2 * r0:2 * (r0 + n), :].astype(F32)).astype(BF)
            for r in range(2):
                csend[i, r, r0:r0 + n, :] = val[r * n:(r + 1) * n]
            ccopy(ph, i, xh).start()
            return carry
        lax.fori_loop(0, 2, step, 0)

    def pv(ci, sc, mrow):
        cols = slice(ci * CK, (ci + 1) * CK)
        p = jnp.exp2(sc[:, cols] - mrow).astype(BF)
        acc[...] += jnp.dot(p, vx[cols, :], preferred_element_type=F32)

    def tile(quart, half, final=False):
        mrow = jnp.max(mx[...], axis=1, keepdims=True)
        acc[...] = jnp.zeros((TQ, 2 * HD), F32)
        if not final:
            prep(quart + half, 1 - half)
        for ci in range(KEYS // CK):
            if not final:
                qk(slice(ci * CK, (ci + 1) * CK), scs[1 - half])
            pv(ci, scs[half], mrow)
        o = (acc[:, :HD] / acc[:, HD:]).astype(BF)
        rows = pl.ds(pl.multiple_of(quart * QUART, QUART), QUART)
        obuf[half * 8:half * 8 + 8, rows, :] = o.reshape(8, QUART, HD)

    def quarter(quart, carry):
        @pl.when(active)
        def _():
            tile(quart, 0)

        @pl.when(quart == 2)
        def _():
            give(0)

        @pl.when(active)
        def _():
            tile(quart, 1)

            @pl.when(quart == 0)
            def _():
                give_back(0, 0, 16)

            @pl.when(quart == 2)
            def _():
                give_back(1, 0, 16)
        return carry
    lax.fori_loop(0, 3, quarter, 0)
    take(0)

    @pl.when(active)
    def _():
        tile(3, 0)
        give_back(2, 0, 8)
        tile(3, 1, True)
        give_back(2, 8, 8)
    give(1)
    take(1)
    for i in range(1, 4):
        for n, (src, dst) in enumerate(((ck_ref, st1k), (cv_ref, st1v))):
            st1(i, src, dst, n).wait_send()
    sent(lambda n: kall.at[0:n * 32, :], 14, ck_ss)
    sent(lambda n: kall.at[0:n * 32, :], 14, cv_ss)
    for b in range(len(PARTS)):
        sent(lambda n: qland.at[0:n, pl.ds(*PARTS[b]), :], 14, q_ss.at[b])
    give(2)
    take(2)

    @pl.when(active)
    def _():
        for ph in range(len(PHASES)):
            sent(lambda n: obuf.at[0:n, pl.ds(*PHASES[ph]), :], 16, o_ss.at[ph])
    for ph in range(len(PHASES)):
        for i in range(2):
            pcopy(ph, i).wait_send()
            ccopy(ph, i, xh).wait_send()
    for ph in range(len(PHASES)):
        for i in range(2):
            ccopy(ph, i, i).wait_recv()


def per_device(queries, fine_keys, fine_values, cache_keys, cache_values, prefix_len, out_weight):
    dma = pltpu.SemaphoreType.DMA
    any_spec = pl.BlockSpec(memory_space=pl.ANY)
    halves = pl.pallas_call(
        kernel,
        out_shape=jax.ShapeDtypeStruct((2, 2, TOK, GW), BF),
        in_specs=[any_spec] * 5 + [pl.BlockSpec(memory_space=pltpu.SMEM), any_spec],
        out_specs=any_spec,
        scratch_shapes=[
            pltpu.VMEM((4, 16, GW), BF), pltpu.VMEM((4, 16, GW), BF),
            pltpu.VMEM((2, 32, GW), BF), pltpu.VMEM((2, 32, GW), BF),
            pltpu.VMEM((KEYS, HD), BF), pltpu.VMEM((KEYS, 2 * HD), BF),
            pltpu.VMEM((2 * HD, KEYS), BF), pltpu.VMEM((SLOTS, TOK, HD), BF),
            pltpu.VMEM((TQ, KEYS), F32), pltpu.VMEM((TQ, KEYS), F32),
            pltpu.VMEM((TQ, 2 * HD), BF), pltpu.VMEM((TQ, HD), F32),
            pltpu.VMEM((TQ, 2 * HD), F32), pltpu.VMEM((SLOTS, TOK, HD), BF),
            pltpu.VMEM((2, TOK, GW), BF), pltpu.VMEM((GW, 4 * GW), BF),
            pltpu.VMEM((2, 2 * TOK, GW), BF), pltpu.VMEM((2, 2 * TOK, GW), BF),
            pltpu.VMEM((2, 2, TOK, GW), BF),
            dma((2, 4)), dma((2, 4)), dma, dma((4,)), dma, dma((4,)),
            dma((3,)), dma((3, 2)), dma((4,)), dma((4,)), dma((4,)), dma((4,)),
            dma, dma, dma, dma, dma((2,)), dma((2,)),
            dma((3,)), dma((3,)), dma((3, 2)), dma((3, 2)), dma((3, 2)), dma((3, 2)), dma,
        ],
        compiler_params=pltpu.CompilerParams(
            collective_id=0, has_side_effects=True, vmem_limit_bytes=58 * 2**20),
        cost_estimate=pl.CostEstimate(flops=7_000_000_000, bytes_accessed=12_000_000, transcendentals=10_000_000),
    )(queries, fine_keys, fine_values, cache_keys.reshape(16, 4 * GW),
      cache_values.reshape(16, 4 * GW), prefix_len, out_weight)
    return (halves[0].astype(F32) + halves[1].astype(F32)).astype(BF)


def solution(mesh):
    return jax.shard_map(
        per_device,
        mesh=mesh,
        in_specs=(
            P(None, "seq", "head"),
            P(None, "seq", "head"),
            P(None, "seq", "head"),
            P(None, ("seq", "head"), None),
            P(None, ("seq", "head"), None),
            P(),
            P("head", None),
        ),
        out_specs=P(None, "seq", "head"),
        check_vma=False,
    )
```

```python
import functools

import jax
import jax.numpy as jnp
from jax import lax
from jax.experimental import pallas as pl
from jax.experimental.pallas import tpu as pltpu
from jax.sharding import PartitionSpec as P

MESH = pl.DeviceIdType.MESH
F32, BF = jnp.float32, jnp.bfloat16
HD = 128
HEADS = 7
GW = HEADS * HD
TOK = 128
COARSE = 1024
KEYS = 5120
TQ = 256
CK = 1024
SLOTS = 16
QUART = TOK // 4
PARTS = ((0, 32), (32, 32), (64, 64))
PHASES = ((0, 32), (32, 64), (96, 32))
LOG2 = float(HD ** -0.5 * 1.4426950408889634)


def rcopy(src, dst, ssem, rsem, s, g):
    return pltpu.make_async_remote_copy(
        src_ref=src, dst_ref=dst, send_sem=ssem, recv_sem=rsem,
        device_id=(s, g), device_id_type=MESH)


def kernel(q_ref, fk_ref, fv_ref, ck_ref, cv_ref, plen_ref, w_ref, out_ref,
           st1k, st1v, st2k, st2v, kall, vx, kt, qland, sc0, sc1, qx, mx, acc, obuf, att, wv,
           psend, precv, csend,
           st1_ss, st1_rs, k_ss, k_rs, v_ss, v_rs, q_ss, q_rs, fk_ss, fk_rs, fv_ss, fv_rs,
           ck_ss, ck_rs, cv_ss, cv_rs, cf_ss, cf_rs, o_ss, o_rs, p_ss, p_rs, c_ss, c_rs, w_sem):
    s = lax.axis_index("seq")
    g = lax.axis_index("head")
    z, xl, y = s >> 3, (s >> 2) & 1, s & 3
    xh, c = g >> 1, g & 1
    zk = z >> 1
    land = y & 1
    sib = xh * 2 + 1 - c
    flip = z * 8 + (1 - xl) * 4 + y

    def place(zd, pos):
        return (pos + 8 - 2 * zd) & 7

    def dest(j):
        zb, xb, yb = j >> 3, (j >> 2) & 1, j & 3
        r = (z + zb) & 1
        zd = 2 * c + r
        pos = ((xl + xb) & 1) * 4 + ((y + yb) & 3)
        h = place(zd, pos)
        sd = zd * 8 + pos
        mine = jnp.logical_and(sd == s, land == c)
        return r, h, sd, mine

    my_r = z & 1
    my_h = place(z, xl * 4 + y)
    active = my_h < HEADS

    def slot_of(j):
        return (z >> 1) * 8 + (j >> 3) * 4 + ((j >> 2) & 1) * 2 + ((j & 3) >> 1)

    def source(slot):
        zs = (slot >> 3) * 2 + ((my_r + (slot >> 2)) & 1)
        yb = (slot & 1) * 2 + ((y + c) & 1)
        return zs, (xl + (slot >> 1)) & 1, (y + 4 - yb) & 3

    barrier = pltpu.get_barrier_semaphore()
    gd = xh * 2 + land
    go = xh * 2 + zk

    def greet(sp, gp, maybe_here):
        def signal():
            pl.semaphore_signal(barrier, inc=1, device_id=(sp, gp), device_id_type=MESH)
        if maybe_here:
            pl.when(jnp.logical_not(jnp.logical_and(sp == s, gp == g)))(signal)
        else:
            signal()
    for j in range(15, -1, -1):
        greet(dest(j)[2], gd, j & 7 == 0)
        zs, xs, ys = source(j)
        greet(zs * 8 + xs * 4 + ys, go, j & 3 == 0)
    own = jnp.logical_and(zk == c, land == c)
    for i in range(1, 4):
        pl.semaphore_signal(barrier, inc=1, device_id=(s, (g + i) & 3), device_id_type=MESH)
    for i in range(2):
        pl.semaphore_signal(barrier, inc=1, device_id=(flip, i * 2 + c), device_id_type=MESH)
    wcopy = pltpu.make_async_copy(w_ref, wv, w_sem)
    wcopy.start()
    vx[:, HD:] = jnp.ones((KEYS, HD), BF)
    pl.semaphore_wait(barrier, 37 - jnp.where(own, 2, 0))


    def st1(i, src, dst, n):
        gp = (g + i) & 3
        cols = pl.ds(pl.multiple_of(gp * GW, HD), GW)
        if i == 0:
            return pltpu.make_async_copy(src.at[:, cols], dst.at[g], st1_rs.at[n, 0])
        return rcopy(src.at[:, cols], dst.at[g], st1_ss.at[n, i], st1_rs.at[n, i], s, gp)
    first = [st1(i, src, dst, n) for i in range(4)
             for n, (src, dst) in enumerate(((ck_ref, st1k), (cv_ref, st1v)))]
    for f in first:
        f.start()

    def move(src, dst, ss, rs, sd, mine, gd=gd):
        @pl.when(mine)
        def _():
            pltpu.make_async_copy(src, dst, rs).start()

        @pl.when(jnp.logical_not(mine))
        def _():
            rcopy(src, dst, ss, rs, sd, gd).start()

    has_mine = jnp.logical_and(own, active)

    def sent(piece, n, sem):
        @pl.when(has_mine)
        def _():
            rcopy(piece(n - 1), piece(n - 1), sem, sem, s, sib).wait_send()

        @pl.when(jnp.logical_not(has_mine))
        def _():
            rcopy(piece(n), piece(n), sem, sem, s, sib).wait_send()

    def came(piece, sem):
        rcopy(piece, piece, sem, sem, s, sib).wait_recv()

    def hcols(h):
        return pl.ds(pl.multiple_of(h * HD, HD), HD)

    def krows(slot, n=1):
        return pl.ds(pl.multiple_of(COARSE + slot * TOK, TOK), n * TOK)

    def kv_args(j):
        r, h, sd, mine = dest(j)
        slot = slot_of(j)
        rows = krows(land * 16 + slot)
        return (h, (fk_ref.at[r, :, hcols(h)], kall.at[rows, :], k_ss, k_rs.at[slot >> 2], sd, mine),
                (fv_ref.at[r, :, hcols(h)], vx.at[rows, 0:HD], v_ss, v_rs.at[slot >> 2], sd, mine))

    def q_args(part):
        rows = pl.ds(*PARTS[part])

        def args(j):
            r, h, sd, mine = dest(j)
            slot = slot_of(j)
            return h, (q_ref.at[r, rows, hcols(h)], qland.at[slot, rows, :],
                       q_ss.at[part], q_rs.at[part, slot >> 3], sd, mine)
        return args

    def c_args(j):
        r, h, sd, mine = dest(j)
        spot = land * 16 + z * 4 + xl * 2 + (y >> 1)
        rows = pl.ds(pl.multiple_of(spot * 32, 32), 32)
        return (h, (st2k.at[r, :, hcols(h)], kall.at[rows, :], ck_ss, ck_rs, sd, mine),
                (st2v.at[r, :, hcols(h)], vx.at[rows, 0:HD], cv_ss, cv_rs, sd, mine))

    def each(args, what):
        def step(j, carry):
            h, *copies = args(j)

            @pl.when(h < HEADS)
            def _():
                for a in copies:
                    what(*a)
            return carry
        lax.fori_loop(0, 16, step, 0)

    for j in range(15, -1, -1):
        h, *copies = kv_args(j)

        @pl.when(h < HEADS)
        def _():
            for src, dst, ss, rs, sd, mine in copies:
                if j & 7 == 0:
                    move(src, dst, ss, rs, sd, mine)
                else:
                    rcopy(src, dst, ss, rs, sd, gd).start()

    for i in range(4):
        for n, (src, dst) in enumerate(((ck_ref, st1k), (cv_ref, st1v))):
            if i == 0:
                st1(0, src, dst, n).wait()
            else:
                st1(i, src, dst, n).wait_recv()
    for r in range(2):
        for a in range(2):
            for src, dst in ((st1k, st2k), (st1v, st2v)):
                lo = src[2 * a].astype(F32)[r * 8:r * 8 + 8]
                hi = src[2 * a + 1].astype(F32)[r * 8:r * 8 + 8]
                dst[r, a * 16:a * 16 + 16, :] = jnp.concatenate([lo, hi], axis=0).astype(BF)
    each(c_args, move)
    each(q_args(0), move)

    ohead = pl.multiple_of(my_h * HD, HD)

    def o_args(ph, j):
        zs, xs, ys = source(j)
        so = zs * 8 + (1 - xs) * 4 + ys
        rows = pl.ds(*PHASES[ph])
        mine = jnp.logical_and(so == s, zk == c)
        return (obuf.at[j, rows, :], att.at[my_r, rows, pl.ds(ohead, HD)], o_ss.at[ph],
                o_rs.at[ph], so, mine, go)

    def give_back(ph, first, count):
        def step(j, carry):
            move(*o_args(ph, j))
            return carry
        lax.fori_loop(first, first + count, step, 0)

    def fwd(ref_k, ss, rs, i, owner, is_v):
        rows = krows(owner * 16 + i * 4, 4)
        piece = ref_k.at[rows, 0:HD] if is_v else ref_k.at[rows, :]
        return rcopy(piece, piece, ss.at[i], rs.at[i], s, sib)

    def cfwd(ref_k, n, owner, is_v):
        rows = pl.ds(pl.multiple_of(owner * 512, 512), 512)
        piece = ref_k.at[rows, 0:HD] if is_v else ref_k.at[rows, :]
        return rcopy(piece, piece, cf_ss.at[n], cf_rs.at[n], s, sib)

    def transpose(row):
        for b in range(2):
            rows = pl.ds(pl.multiple_of(row + b * 256, 256), 256)
            kk = kall[rows, :].T
            kt[0:HD, rows] = kk
            kt[HD:, rows] = kk

    @pl.when(active)
    def _():
        def landed(n, carry):
            i = (n & 1) * 2 + 1 - (n >> 1)
            rows = krows(c * 16 + i * 4, 4)
            came(kall.at[rows, :], k_rs.at[i])
            fwd(kall, fk_ss, fk_rs, i, c, False).start()
            came(vx.at[rows, 0:HD], v_rs.at[i])
            fwd(vx, fv_ss, fv_rs, i, c, True).start()
            return carry
        lax.fori_loop(0, 4, landed, 0)
        rows = pl.ds(pl.multiple_of(c * 512, 512), 512)
        came(kall.at[rows, :], ck_rs)
        cfwd(kall, 0, c, False).start()
        came(vx.at[rows, 0:HD], cv_rs)
        cfwd(vx, 1, c, True).start()

    sent(lambda n: kall.at[0:n * TOK, :], 14, k_ss)
    sent(lambda n: kall.at[0:n * TOK, :], 14, v_ss)
    each(q_args(1), move)
    each(q_args(2), move)

    scs = (sc0, sc1)

    def prep(quart, half):
        slots = pl.ds(half * 8, 8)

        for b in range(len(PARTS)):
            @pl.when(quart == PARTS[b][0] // QUART)
            def _():
                came(qland.at[slots, pl.ds(*PARTS[b]), :], q_rs.at[b, half])
        rows = pl.ds(pl.multiple_of(quart * QUART, QUART), QUART)
        x = qland[half * 8:half * 8 + 8, rows, :].reshape(TQ, HD).astype(F32) * LOG2
        hi = x.astype(BF)
        qx[:, :HD] = hi
        qx[:, HD:] = (x - hi.astype(F32)).astype(BF)
        mx[...] = jnp.full((TQ, HD), -jnp.inf, F32)

    def qk(cols, sc):
        val = jnp.dot(qx[...], kt[:, cols], preferred_element_type=F32)
        sc[:, cols] = val
        m = mx[...]
        for b in range(CK // HD):
            m = jnp.maximum(m, val[:, b * HD:(b + 1) * HD])
        mx[...] = m

    @pl.when(active)
    def _():
        def mine_t(i, carry):
            transpose(COARSE + c * 2048 + i * 512)
            return carry
        lax.fori_loop(0, 4, mine_t, 0)
        prep(0, 0)

        def early(owner):
            def step(i, carry):
                qk(pl.ds(pl.multiple_of(COARSE + owner * 2048 + i * CK, CK), CK), sc0)
                return carry
            lax.fori_loop(0, 2, step, 0)
        early(c)

        def theirs_t(n, carry):
            i = (n & 1) * 2 + 1 - (n >> 1)
            fwd(kall, fk_ss, fk_rs, i, 1 - c, False).wait_recv()
            transpose(COARSE + (1 - c) * 2048 + i * 512)
            return carry
        lax.fori_loop(0, 4, theirs_t, 0)
        early(1 - c)

        def theirs_v(i, carry):
            fwd(vx, fv_ss, fv_rs, i, 1 - c, True).wait_recv()
            fwd(kall, fk_ss, fk_rs, i, c, False).wait_send()
            fwd(vx, fv_ss, fv_rs, i, c, True).wait_send()
            return carry
        lax.fori_loop(0, 4, theirs_v, 0)
        cfwd(kall, 0, 1 - c, False).wait_recv()
        cfwd(vx, 1, 1 - c, True).wait_recv()
        cfwd(kall, 0, c, False).wait_send()
        cfwd(vx, 1, c, True).wait_send()

        plen = plen_ref[my_r]
        k0 = kall[COARSE:COARSE + 1, :].astype(F32)
        row = lax.broadcasted_iota(jnp.int32, (256, HD), 0)
        token = 512 + (row >> 6) * 128 + ((row >> 5) & 1) * 64 + (row & 31)
        for i in range(4):
            rows = slice(i * 256, (i + 1) * 256)
            kk = kall[rows, :]
            if i % 2 == 1:
                seen = token + (i // 2) * 32 < plen
                kk = jnp.where(seen, kk.astype(F32), k0).astype(BF)
                vx[rows, 0:HD] = jnp.where(seen, vx[rows, 0:HD].astype(F32), 0.0).astype(BF)
                vx[rows, HD:] = jnp.where(seen, 1.0, 0.0).astype(BF)
            kk = kk.T
            kt[0:HD, rows] = kk
            kt[HD:, rows] = kk
        qk(slice(0, COARSE), sc0)

    def part(ph, gp):
        r0, n = PHASES[ph]
        rows = jnp.concatenate([att[0, r0:r0 + n, :], att[1, r0:r0 + n, :]], axis=0)
        cols = pl.ds(pl.multiple_of(gp * GW, HD), GW)
        return jnp.dot(rows, wv[:, cols], preferred_element_type=F32)

    def pcopy(ph, i):
        rows = pl.ds(2 * PHASES[ph][0], 2 * PHASES[ph][1])
        return rcopy(psend.at[i, rows, :], precv.at[i, rows, :], p_ss.at[ph, i], p_rs.at[ph, i], s, sib)

    def ccopy(ph, i, half):
        rows = pl.ds(*PHASES[ph])
        return rcopy(csend.at[i, :, rows, :], out_ref.at[half, :, rows, :], c_ss.at[ph, i],
                     c_rs.at[ph, half], flip, i * 2 + c)

    def give(ph):
        r0, n = PHASES[ph]

        came(att.at[:, pl.ds(r0, n), :], o_rs.at[ph])
        if ph == 0:
            wcopy.wait()

        def step(i, carry):
            psend[i, 2 * r0:2 * (r0 + n), :] = part(ph, i * 2 + 1 - c).astype(BF)
            pcopy(ph, i).start()
            return carry
        lax.fori_loop(0, 2, step, 0)

    def take(ph):
        r0, n = PHASES[ph]

        def step(i, carry):
            val = part(ph, i * 2 + c)
            pcopy(ph, i).wait_recv()
            val = (val + precv[i, 2 * r0:2 * (r0 + n), :].astype(F32)).astype(BF)
            for r in range(2):
                csend[i, r, r0:r0 + n, :] = val[r * n:(r + 1) * n]
            ccopy(ph, i, xh).start()
            return carry
        lax.fori_loop(0, 2, step, 0)

    def pv(ci, sc, mrow):
        cols = slice(ci * CK, (ci + 1) * CK)
        p = jnp.exp2(sc[:, cols] - mrow).astype(BF)
        acc[...] += jnp.dot(p, vx[cols, :], preferred_element_type=F32)

    def tile(quart, half, final=False):
        mrow = jnp.max(mx[...], axis=1, keepdims=True)
        acc[...] = jnp.zeros((TQ, 2 * HD), F32)
        if not final:
            prep(quart + half, 1 - half)
        for ci in range(KEYS // CK):
            if not final:
                qk(slice(ci * CK, (ci + 1) * CK), scs[1 - half])
            pv(ci, scs[half], mrow)
        o = (acc[:, :HD] / acc[:, HD:]).astype(BF)
        rows = pl.ds(pl.multiple_of(quart * QUART, QUART), QUART)
        obuf[half * 8:half * 8 + 8, rows, :] = o.reshape(8, QUART, HD)

    def quarter(quart, carry):
        @pl.when(active)
        def _():
            tile(quart, 0)

        @pl.when(quart == 2)
        def _():
            give(0)

        @pl.when(active)
        def _():
            tile(quart, 1)

            @pl.when(quart == 0)
            def _():
                give_back(0, 0, 16)

            @pl.when(quart == 2)
            def _():
                give_back(1, 0, 16)
        return carry
    lax.fori_loop(0, 3, quarter, 0)
    take(0)

    @pl.when(active)
    def _():
        tile(3, 0)
        give_back(2, 0, 8)
        tile(3, 1, True)
        give_back(2, 8, 8)
    give(1)
    take(1)
    for i in range(1, 4):
        for n, (src, dst) in enumerate(((ck_ref, st1k), (cv_ref, st1v))):
            st1(i, src, dst, n).wait_send()
    sent(lambda n: kall.at[0:n * 32, :], 14, ck_ss)
    sent(lambda n: kall.at[0:n * 32, :], 14, cv_ss)
    for b in range(len(PARTS)):
        sent(lambda n: qland.at[0:n, pl.ds(*PARTS[b]), :], 14, q_ss.at[b])
    give(2)
    take(2)

    @pl.when(active)
    def _():
        for ph in range(len(PHASES)):
            sent(lambda n: obuf.at[0:n, pl.ds(*PHASES[ph]), :], 16, o_ss.at[ph])
    for ph in range(len(PHASES)):
        for i in range(2):
            pcopy(ph, i).wait_send()
            ccopy(ph, i, xh).wait_send()
    for ph in range(len(PHASES)):
        for i in range(2):
            ccopy(ph, i, i).wait_recv()


def per_device(queries, fine_keys, fine_values, cache_keys, cache_values, prefix_len, out_weight):
    dma = pltpu.SemaphoreType.DMA
    any_spec = pl.BlockSpec(memory_space=pl.ANY)
    halves = pl.pallas_call(
        kernel,
        out_shape=jax.ShapeDtypeStruct((2, 2, TOK, GW), BF),
        in_specs=[any_spec] * 5 + [pl.BlockSpec(memory_space=pltpu.SMEM), any_spec],
        out_specs=any_spec,
        scratch_shapes=[
            pltpu.VMEM((4, 16, GW), BF), pltpu.VMEM((4, 16, GW), BF),
            pltpu.VMEM((2, 32, GW), BF), pltpu.VMEM((2, 32, GW), BF),
            pltpu.VMEM((KEYS, HD), BF), pltpu.VMEM((KEYS, 2 * HD), BF),
            pltpu.VMEM((2 * HD, KEYS), BF), pltpu.VMEM((SLOTS, TOK, HD), BF),
            pltpu.VMEM((TQ, KEYS), F32), pltpu.VMEM((TQ, KEYS), F32),
            pltpu.VMEM((TQ, 2 * HD), BF), pltpu.VMEM((TQ, HD), F32),
            pltpu.VMEM((TQ, 2 * HD), F32), pltpu.VMEM((SLOTS, TOK, HD), BF),
            pltpu.VMEM((2, TOK, GW), BF), pltpu.VMEM((GW, 4 * GW), BF),
            pltpu.VMEM((2, 2 * TOK, GW), BF), pltpu.VMEM((2, 2 * TOK, GW), BF),
            pltpu.VMEM((2, 2, TOK, GW), BF),
            dma((2, 4)), dma((2, 4)), dma, dma((4,)), dma, dma((4,)),
            dma((3,)), dma((3, 2)), dma((4,)), dma((4,)), dma((4,)), dma((4,)),
            dma, dma, dma, dma, dma((2,)), dma((2,)),
            dma((3,)), dma((3,)), dma((3, 2)), dma((3, 2)), dma((3, 2)), dma((3, 2)), dma,
        ],
        compiler_params=pltpu.CompilerParams(
            collective_id=0, has_side_effects=True, vmem_limit_bytes=58 * 2**20),
        cost_estimate=pl.CostEstimate(flops=7_000_000_000, bytes_accessed=12_000_000, transcendentals=10_000_000),
    )(queries, fine_keys, fine_values, cache_keys.reshape(16, 4 * GW),
      cache_values.reshape(16, 4 * GW), prefix_len, out_weight)
    return (halves[0].astype(F32) + halves[1].astype(F32)).astype(BF)


def solution(mesh):
    return jax.shard_map(
        per_device,
        mesh=mesh,
        in_specs=(
            P(None, "seq", "head"),
            P(None, "seq", "head"),
            P(None, "seq", "head"),
            P(None, ("seq", "head"), None),
            P(None, ("seq", "head"), None),
            P(),
            P("head", None),
        ),
        out_specs=P(None, "seq", "head"),
        check_vma=False,
    )
```
